128 devices in a mesh: row: 8 (over x, z_lo), col: 16 (over y, z_hi, core).
Axes of the slice: x: 4, y: 4, z: 4 (z_hi: 2, z_lo: 2; z = z_hi * 2 + z_lo), core: 2. Of those that a mesh axis runs over, the one named last changes fastest.
Arguments:
- pixels: float32 [3, 384, 512], P(None, 'row', 'col'), may hold values from -6 to 6
- stem_weight: bfloat16 [64, 3, 4, 4], replicated, may hold values from -0.875 to 0.875
- first_weight: bfloat16 [64, 64, 3, 3], replicated, may hold values from -0.25 to 0.25
- second_weight: bfloat16 [64, 64, 3, 3], replicated, may hold values from -0.25 to 0.25
- entry_weight: bfloat16 [256, 64, 3, 3], P('col'), may hold values from -0.25 to 0.25
- final_weight: bfloat16 [256, 256, 3, 3], P('col'), may hold values from -0.125 to 0.125
- upstream: bfloat16 [256, 192, 256], P('col', 'row'), may hold values from -6 to 6
Outputs:
- stem_grad: float32 [64, 3, 4, 4], replicated
- first_grad: float32 [64, 64, 3, 3], replicated
- second_grad: float32 [64, 64, 3, 3], replicated
- entry_grad: float32 [256, 64, 3, 3], P('col')
- final_grad: float32 [256, 256, 3, 3], P('col')
The draws below stay inside these ranges and needn't reach their ends.
All inputs are finite; a program needn't handle non-finite values.
Results may differ from the reference program's by a relative error of at most 0.023.
Values may be sent and summed in bfloat16 or wider, within the bound.
No kernel may reach another device: no remote copies, remote signals or barrier semaphores. Data moves between devices by JAX's collectives and lax.ppermute only.
A program may use at most 64 MiB of HBM per device.

```python
import math
import jax
import jax.numpy as jnp
from jax import lax

C_IN = 3
F = 64
G = 256
HH = 192
WW = 256
H = 384
W = 512
G_DEV = 16
N_COL = 16


def block_levels(key, dims, pieces, low, high):
    def one(axis_at, shards_of):
        draws = jax.random.uniform(jax.random.fold_in(jax.random.fold_in(key, 6), axis_at), (shards_of,), jnp.float32, low / len(pieces), high / len(pieces))
        return jnp.repeat(jnp.exp(draws), dims[axis_at] // shards_of).reshape((-1,) + (1,) * (len(dims) - axis_at - 1))

    level = one(*pieces[0])
    for cut in pieces[1:]:
        level = level * one(*cut)
    return level


def scatter_about(own_key, extent, scale, reach, shards=(), kind=jnp.bfloat16):
    array = scale * jax.random.normal(own_key, extent, jnp.float32)
    if shards:
        array = array * block_levels(own_key, extent, shards, -0.22, 0.18)
    return jnp.clip(array, -reach, reach).astype(kind)


def setup_inputs(seed: int = 0) -> dict:
    streams_of = jax.random.split(jax.random.key(seed), 8)
    return {
        "pixels": scatter_about(streams_of[0], (C_IN, H, W), 1.0, 6.0, ((1, 8), (2, 16)), jnp.float32),
        "stem_weight": scatter_about(streams_of[1], (F, C_IN, 4, 4), (C_IN * 16) ** -0.5, 0.875),
        "first_weight": scatter_about(streams_of[2], (F, F, 3, 3), (F * 9) ** -0.5, 0.25),
        "second_weight": scatter_about(streams_of[3], (F, F, 3, 3), (F * 9) ** -0.5, 0.25),
        "entry_weight": scatter_about(streams_of[4], (G, F, 3, 3), (F * 9) ** -0.5, 0.25, ((0, 16),)),
        "final_weight": scatter_about(streams_of[5], (G, G, 3, 3), (G * 9) ** -0.5, 0.125, ((0, 16),)),
        "upstream": scatter_about(streams_of[6], (G, HH, WW), 1.0, 6.0, ((0, 16), (1, 8))),
    }


def conv_valid(field, kernel, stride):
    return lax.conv_general_dilated(field[None], kernel, (stride, stride), 'VALID', dimension_numbers=('NCHW', 'OIHW', 'NCHW'), preferred_element_type=jnp.float32)[0]

def weight_grad(padded, upstream, stride):
    result = lax.conv_general_dilated(padded[:, None], upstream[:, None], (1, 1), 'VALID', rhs_dilation=(stride, stride), dimension_numbers=('NCHW', 'OIHW', 'NCHW'), preferred_element_type=jnp.float32)
    return result.transpose(1, 0, 2, 3)

def back_kernel(kernel):
    return jnp.flip(kernel, (2, 3)).transpose(1, 0, 2, 3)

def silu_slope(values):
    logistic = jax.nn.sigmoid(values)
    return logistic * (1.0 + values * (1.0 - logistic))

def border(field):
    return jnp.pad(field, ((0, 0), (1, 1), (1, 1)))

def reference(pixels, stem_weight, first_weight, second_weight, entry_weight, final_weight, upstream):
    norm_scale = 1.0 / math.sqrt(HH * WW)
    inputs = pixels.astype(jnp.bfloat16)
    padded_in = border(inputs)
    stem_pre = conv_valid(padded_in, stem_weight, 2)
    stem_act = border(jax.nn.silu(stem_pre).astype(jnp.bfloat16))
    first_pre = conv_valid(stem_act, first_weight, 1)
    first_act = border(jax.nn.silu(first_pre).astype(jnp.bfloat16))
    second_pre = conv_valid(first_act, second_weight, 1)
    second_act = border(jax.nn.silu(second_pre).astype(jnp.bfloat16))
    entry_pre = conv_valid(second_act, entry_weight, 1)
    entry_act = border(jax.nn.silu(entry_pre).astype(jnp.bfloat16))
    final_grad = weight_grad(entry_act, upstream, 1)
    groups_kernel = final_weight.reshape(N_COL, G_DEV, G, 3, 3)
    groups_up = border(upstream).reshape(N_COL, G_DEV, HH + 2, WW + 2)

    def add_group(running, member):
        partial_value = conv_valid(member[1], back_kernel(member[0]), 1).astype(jnp.bfloat16)
        partial_value = lax.optimization_barrier(partial_value)
        return (running + partial_value.astype(jnp.float32), None)
    entry_back, ignored = lax.scan(add_group, jnp.zeros((G, HH, WW), jnp.float32), (groups_kernel, groups_up))
    entry_delta = (entry_back * silu_slope(entry_pre)).astype(jnp.bfloat16)
    entry_grad = weight_grad(second_act, entry_delta, 1)
    second_back = conv_valid(border(entry_delta), back_kernel(entry_weight), 1)
    second_delta = (second_back * silu_slope(second_pre)).astype(jnp.bfloat16)
    second_grad = weight_grad(first_act, second_delta, 1)
    first_back = conv_valid(border(second_delta), back_kernel(second_weight), 1)
    first_delta = (first_back * silu_slope(first_pre)).astype(jnp.bfloat16)
    first_grad = weight_grad(stem_act, first_delta, 1)
    stem_back = conv_valid(border(first_delta), back_kernel(first_weight), 1)
    stem_delta = (stem_back * silu_slope(stem_pre)).astype(jnp.bfloat16)
    stem_grad = weight_grad(padded_in, stem_delta, 2)
    return (stem_grad * norm_scale, first_grad * norm_scale, second_grad * norm_scale, entry_grad * norm_scale, final_grad * norm_scale)
```

```python
import functools
import math

import jax
import jax.numpy as jnp
from jax import lax
from jax.experimental import pallas as pl
from jax.experimental.pallas import tpu as pltpu
from jax.sharding import PartitionSpec as P

BF = jnp.bfloat16
F32 = jnp.float32

TILE_H, TILE_W = 24, 16
HALO = 7
FRAME_H = TILE_H + 2 * HALO
FRAME_W = 32
CELLS = FRAME_H * FRAME_W
UP_H = TILE_H + 8
F = 64
G = 256
GD = 16
L_FINAL = 9 * G
L_ENTRY = 640
L_UP = UP_H * FRAME_W
L_SEND = L_FINAL + L_ENTRY + L_UP
L_STEM = 384
L_GRAD = L_FINAL + L_ENTRY + L_STEM

NT = (((1,), (1,)), ((), ()))
NN = (((1,), (0,)), ((), ()))
TN = (((0,), (0,)), ((), ()))


def dot(a, b, dims):
    return lax.dot_general(a, b, dims, preferred_element_type=F32)


def pack_kernel(up_ref, final_ref, entry_ref, out_ref, entry_row):
    n_col = out_ref.shape[0]
    entry_row[...] = jnp.zeros_like(entry_row)
    for t in range(9):
        out_ref[:, :, t * G : (t + 1) * G] = jnp.broadcast_to(final_ref[t][None], (n_col, GD, G))
        entry_row[:, t * F : (t + 1) * F] = entry_ref[t].astype(F32)
    out_ref[:, :, L_FINAL : L_FINAL + L_ENTRY] = jnp.broadcast_to(
        entry_row[...].astype(BF)[None], (n_col, GD, L_ENTRY)
    )
    cols = up_ref.shape[2]
    lanes = n_col * 128
    lane = lax.broadcasted_iota(jnp.int32, (cols, lanes), 1)
    col = lax.broadcasted_iota(jnp.int32, (cols, lanes), 0)
    want = (lane >> 7) * TILE_W - HALO + (lane & 31)
    hit = want == col
    block = (lane >> 5) & 3
    total = None
    for m in range(4):
        pick = jnp.where(hit & (block == m), 1.0, 0.0).astype(BF)
        rows = jnp.concatenate([up_ref[4 * k + m] for k in range(UP_H // 4)], axis=0)
        part = dot(rows, pick, NN)
        total = part if total is None else total + part
    total = total.astype(BF)
    for k in range(UP_H // 4):
        for d in range(n_col):
            start = L_FINAL + L_ENTRY + 128 * k
            out_ref[d, :, start : start + 128] = total[k * GD : (k + 1) * GD, 128 * d : 128 * (d + 1)]


def px(first, last):
    return slice(first * FRAME_W, last * FRAME_W)


def main_kernel(
    n_row,
    pos_ref,
    pix_ref,
    w0_ref,
    w1_ref,
    w2_ref,
    recv_ref,
    out_ref,
    valid,
    own,
    x0,
    x1,
    x2,
    x3,
    e3,
    up,
    k1,
    k2,
    k3,
    s1,
    s2,
    s3,
    s4,
    d4,
    d3,
    d2,
    wide,
    stem_out,
):
    n_col = recv_ref.shape[0]
    cell = lax.broadcasted_iota(jnp.int32, (CELLS, 128), 0)
    row = (cell >> 5) - HALO + pos_ref[0] * TILE_H
    col_in = (cell & 31) - HALO
    col = col_in + pos_ref[1] * TILE_W
    inside = (row >= 0) & (row < n_row * TILE_H) & (col >= 0) & (col < n_col * TILE_W)
    valid[...] = jnp.where(inside, 1.0, 0.0)
    own[...] = jnp.where((col_in >= 0) & (col_in < TILE_W), 1.0, 0.0)

    def three(ref, first, last, value, width):
        n = value.shape[0]
        ref[px(first, last), 0:width] = pltpu.roll(value, 1, 0).astype(BF)
        ref[px(first, last), width : 2 * width] = value.astype(BF)
        ref[px(first, last), 2 * width : 3 * width] = pltpu.roll(value, n - 1, 0).astype(BF)

    def conv(ref, taps, first, last):
        return sum(dot(ref[px(first + p - 1, last + p - 1), :], taps[p], NT) for p in range(3))

    def act(pre, first, last):
        logistic = 1.0 / (1.0 + jnp.exp(-pre))
        width = pre.shape[1]
        mask = valid[px(first, last), :]
        mask = mask[:, :width] if width <= 128 else jnp.concatenate([mask] * (width // 128), axis=1)
        return pre * logistic * mask, logistic * (1.0 + pre * (1.0 - logistic)) * mask

    for p in range(3):
        for q in range(3):
            k1[p, :, q * F : (q + 1) * F] = w1_ref[3 * p + q]
            k2[p, :, q * F : (q + 1) * F] = w2_ref[3 * p + q]
        start = L_FINAL + 3 * F * p
        k3[p] = recv_ref[:, :, start : start + 3 * F].reshape(n_col * GD, 3 * F)

    three(x0, 0, FRAME_H, jnp.transpose(pix_ref[...].astype(F32))[:CELLS], 16)
    a, s = act(conv(x0, [w0_ref[p] for p in range(3)], 1, 37), 1, 37)
    three(x1, 1, 37, a, F)
    s1[...] = s[px(6, 30), :]
    a, s = act(conv(x1, [k1[p] for p in range(3)], 2, 36), 2, 36)
    three(x2, 2, 36, a, F)
    s2[...] = s[px(4, 30), :]
    a, s = act(conv(x2, [k2[p] for p in range(3)], 3, 35), 3, 35)
    three(x3, 3, 35, a, F)
    s3[...] = s[px(2, 30), :]
    a, s = act(conv(x3, [k3[p] for p in range(3)], 4, 34), 4, 34)
    s4[...] = s
    n = a.shape[0]
    e3[0] = pltpu.roll(a, 1, 0).astype(BF)
    e3[1] = a.astype(BF)
    e3[2] = pltpu.roll(a, n - 1, 0).astype(BF)

    up_t = recv_ref[:, :, L_FINAL + L_ENTRY :].reshape(n_col * GD, L_UP)
    lane = lax.broadcasted_iota(jnp.int32, (n_col * GD, TILE_H * FRAME_W), 1) & 31
    mine = (lane >= HALO) & (lane < HALO + TILE_W)
    up_own = jnp.where(mine, up_t[:, 4 * FRAME_W : 28 * FRAME_W].astype(F32), 0.0).astype(BF)
    for p in range(3):
        for q in range(3):
            grad = dot(up_own, e3[q, px(2 + p, 26 + p), :], NN)
            start = (3 * p + q) * G
            out_ref[:, :, start : start + G] = grad.astype(BF).reshape(n_col, GD, G)

    up[...] = jnp.transpose(up_t.astype(F32)).astype(BF)
    back = None
    for q in range(3):
        part = None
        for p in range(3):
            start = (3 * p + q) * G
            kernel = recv_ref[:, :, start : start + G].reshape(n_col * GD, G)
            term = dot(up[px(2 - p, 32 - p), :], kernel, NN)
            part = term if part is None else part + term
        if q != 1:
            part = pltpu.roll(part, n - 1 if q == 0 else 1, 0)
        back = part if back is None else back + part
    d4[...] = (back * s4[...]).astype(BF)

    def masked(ref, offset):
        delta = ref[px(7 - offset, 31 - offset), :].astype(F32)
        mask = own[px(7, 31), :]
        width = delta.shape[1]
        mask = mask[:, :width] if width <= 128 else jnp.concatenate([mask] * (width // 128), axis=1)
        return (delta * mask).astype(BF)

    def grads(delta, ref):
        return [dot(delta, ref[px(6 + p, 30 + p), :], TN) for p in range(3)]

    def back_conv(ref, offset, taps, first, last):
        count = (last - first) * FRAME_W
        wide[0:count, :] = sum(
            dot(ref[px(first - p + 1 - offset, last - p + 1 - offset), :], taps[p], NN) for p in range(3)
        )
        return (
            pltpu.roll(wide[0:count, 0:F], count - 1, 0)
            + wide[0:count, F : 2 * F]
            + pltpu.roll(wide[0:count, 2 * F : 3 * F], 1, 0)
        )

    for p, grad in enumerate(grads(masked(d4, 4), x3)):
        start = L_FINAL + 3 * F * p
        out_ref[:, :, start : start + 3 * F] = grad.astype(BF).reshape(n_col, GD, 3 * F)
    out_ref[:, :, L_FINAL + 9 * F : L_FINAL + L_ENTRY] = jnp.zeros((n_col, GD, L_ENTRY - 9 * F), BF)

    stem_out[...] = jnp.zeros_like(stem_out)
    d3[...] = (back_conv(d4, 4, [k3[p] for p in range(3)], 5, 33) * s3[...]).astype(BF)
    for p, grad in enumerate(grads(masked(d3, 5), x2)):
        stem_out[:, 576 + 192 * p : 768 + 192 * p] = grad
    d2[...] = (back_conv(d3, 5, [k2[p] for p in range(3)], 6, 32) * s2[...]).astype(BF)
    for p, grad in enumerate(grads(masked(d2, 6), x1)):
        stem_out[:, 192 * p : 192 + 192 * p] = grad
    d1 = back_conv(d2, 6, [k1[p] for p in range(3)], 7, 31) * s1[...]
    d1 = d1 * own[px(7, 31), :][:, :F]
    for p, grad in enumerate(grads(d1.astype(BF), x0)):
        stem_out[:, 1152 + 48 * p : 1200 + 48 * p] = grad
    for i in range(4):
        for j in range(4):
            out_ref[4 * i + j, :, L_FINAL + L_ENTRY :] = stem_out[
                16 * i : 16 * (i + 1), L_STEM * j : L_STEM * (j + 1)
            ].astype(BF)


def sum_kernel(in_ref, out_ref):
    total = in_ref[0].astype(F32)
    for d in range(1, in_ref.shape[0]):
        total = total + in_ref[d].astype(F32)
    out_ref[...] = jnp.broadcast_to(total.astype(BF)[None], out_ref.shape)


def tail_kernel(scale, in_ref, final_ref, entry_ref, stem_ref):
    total = in_ref[0].astype(F32)
    for d in range(1, in_ref.shape[0]):
        total = total + in_ref[d].astype(F32)
    total = total * scale
    for t in range(9):
        final_ref[t] = total[:, t * G : (t + 1) * G]
        entry_ref[t] = total[:, L_FINAL + t * F : L_FINAL + (t + 1) * F]
    stem_ref[...] = jnp.broadcast_to(total[:, L_FINAL + L_ENTRY :].astype(BF)[None], stem_ref.shape)


def stem_kernel(in_ref, stem_ref, first_ref, second_ref, whole):
    for i in range(4):
        for j in range(4):
            whole[16 * i : 16 * (i + 1), L_STEM * j : L_STEM * (j + 1)] = in_ref[4 * i + j].astype(F32)
    for t in range(9):
        first_ref[t] = whole[:, t * F : (t + 1) * F]
        second_ref[t] = whole[:, 576 + t * F : 576 + (t + 1) * F]
    for p in range(3):
        stem_ref[p] = whole[:, 1152 + 48 * p : 1200 + 48 * p]


def call(kernel, out_shape, scratch=(), n_in=1, smem=()):
    return pl.pallas_call(
        kernel,
        out_shape=out_shape,
        in_specs=[
            pl.BlockSpec(memory_space=pltpu.SMEM if i in smem else pltpu.VMEM) for i in range(n_in)
        ],
        out_specs=jax.tree.map(lambda _: pl.BlockSpec(memory_space=pltpu.VMEM), out_shape),
        scratch_shapes=list(scratch),
        compiler_params=pltpu.CompilerParams(vmem_limit_bytes=48 * 1024 * 1024),
    )


def rims(block, axis, dim, low, high):
    count = lax.axis_size(axis)
    forward = [(i, i + 1) for i in range(count - 1)]
    backward = [(target, source) for source, target in forward]
    size = block.shape[dim]
    before = lax.ppermute(lax.slice_in_dim(block, size - low, size, axis=dim), axis, forward)
    after = lax.ppermute(lax.slice_in_dim(block, 0, high, axis=dim), axis, backward)
    return jnp.concatenate([before, block, after], axis=dim)


def per_device(
    pixels, stem_weight, first_weight, second_weight, entry_weight, final_weight, upstream
):
    n_row = lax.axis_size("row")
    n_col = lax.axis_size("col")
    shape = jax.ShapeDtypeStruct
    scale = 1.0 / math.sqrt(TILE_H * n_row * TILE_W * n_col)
    pos = jnp.stack([lax.axis_index("row"), lax.axis_index("col")]).astype(jnp.int32)

    cells = pixels.astype(BF).reshape(3, TILE_H, 2, TILE_W, 2).transpose(0, 2, 4, 1, 3)
    cells = cells.reshape(12, TILE_H, TILE_W)
    cells = rims(rims(cells, "row", 1, HALO, HALO), "col", 2, HALO, FRAME_W - TILE_W - HALO)
    cells = jnp.pad(cells.reshape(12, CELLS), ((0, 4), (0, 1280 - CELLS)))

    up_rows = rims(upstream, "row", 1, 4, 4).transpose(1, 0, 2)
    taps = lambda w: w.transpose(2, 3, 0, 1).reshape((9,) + w.shape[:2])
    send = call(
        pack_kernel,
        shape((n_col, GD, L_SEND), BF),
        [pltpu.VMEM((GD, L_ENTRY), F32)],
        3,
    )(up_rows, taps(final_weight), taps(entry_weight))
    recv = lax.all_to_all(send, "col", 0, 0, tiled=True)

    w0 = jnp.pad(stem_weight, ((0, 0), (0, 0), (1, 1), (1, 1))).reshape(F, 3, 3, 2, 3, 2)
    w0 = w0.transpose(2, 0, 4, 1, 3, 5).reshape(3, F, 3, 12)
    w0 = jnp.pad(w0, ((0, 0), (0, 0), (0, 0), (0, 4))).reshape(3, F, 48)

    vmem = pltpu.VMEM
    sends = call(
        functools.partial(main_kernel, n_row),
        shape((n_col, GD, L_GRAD), BF),
        [
            vmem((CELLS, 128), F32),
            vmem((CELLS, 128), F32),
            vmem((CELLS, 48), BF),
            vmem((CELLS, 3 * F), BF),
            vmem((CELLS, 3 * F), BF),
            vmem((CELLS, 3 * F), BF),
            vmem((3, 30 * FRAME_W, G), BF),
            vmem((L_UP, G), BF),
            vmem((3, F, 3 * F), BF),
            vmem((3, F, 3 * F), BF),
            vmem((3, G, 3 * F), BF),
            vmem((24 * FRAME_W, F), F32),
            vmem((26 * FRAME_W, F), F32),
            vmem((28 * FRAME_W, F), F32),
            vmem((30 * FRAME_W, G), F32),
            vmem((30 * FRAME_W, G), BF),
            vmem((28 * FRAME_W, F), BF),
            vmem((26 * FRAME_W, F), BF),
            vmem((28 * FRAME_W, 3 * F), F32),
            vmem((F, 4 * L_STEM), F32),
        ],
        6,
        (0,),
    )(pos, cells, w0, taps(first_weight), taps(second_weight), recv)

    parts = lax.all_to_all(sends, "col", 0, 0, tiled=True)
    band = call(sum_kernel, shape((n_row, GD, L_GRAD), BF))(parts)
    bands = lax.all_to_all(band, "row", 0, 0, tiled=True)
    final_grad, entry_grad, stem_part = call(
        functools.partial(tail_kernel, scale),
        (
            shape((9, GD, G), F32),
            shape((9, GD, F), F32),
            shape((n_col, GD, L_STEM), BF),
        ),
    )(bands)
    stem_all = lax.all_to_all(stem_part, "col", 0, 0, tiled=True)
    stem_grad, first_grad, second_grad = call(
        stem_kernel,
        (shape((3, F, 48), F32), shape((9, F, F), F32), shape((9, F, F), F32)),
        [vmem((F, 4 * L_STEM), F32)],
    )(stem_all)

    untap = lambda g: g.reshape((3, 3) + g.shape[1:]).transpose(2, 3, 0, 1)
    stem_grad = stem_grad.reshape(3, F, 3, 16)[..., :12].reshape(3, F, 3, 3, 2, 2)
    stem_grad = stem_grad.transpose(1, 3, 0, 4, 2, 5).reshape(F, 3, 6, 6)[:, :, 1:5, 1:5]
    return (stem_grad, untap(first_grad), untap(second_grad), untap(entry_grad), untap(final_grad))


def solution(mesh):
    return jax.shard_map(
        per_device,
        mesh=mesh,
        in_specs=(
            P(None, "row", "col"),
            P(),
            P(),
            P(),
            P("col", None, None, None),
            P("col", None, None, None),
            P("col", "row", None),
        ),
        out_specs=(P(), P(), P(), P("col", None, None, None), P("col", None, None, None)),
        check_vma=False,
    )
```

```python
import functools
import math

import jax
import jax.numpy as jnp
from jax import lax
from jax.experimental import pallas as pl
from jax.experimental.pallas import tpu as pltpu
from jax.sharding import PartitionSpec as P

BF = jnp.bfloat16
F32 = jnp.float32

TILE_H, TILE_W = 24, 16
HALO = 7
FRAME_H = TILE_H + 2 * HALO
FRAME_W = 32
CELLS = FRAME_H * FRAME_W
UP_H = TILE_H + 8
F = 64
G = 256
GD = 16
L_FINAL = 9 * G
L_ENTRY = 640
L_UP = UP_H * FRAME_W
L_WEIGHTS = L_FINAL + L_ENTRY
L_SEND = L_WEIGHTS + 2 * L_UP
T_GROUP = L_WEIGHTS // 128
T_STEM = 6
T_Y = 2 * T_GROUP + T_STEM
T_Z = T_GROUP + T_STEM
L_STEM = 384

NT = (((1,), (1,)), ((), ()))
NN = (((1,), (0,)), ((), ()))
TN = (((0,), (0,)), ((), ()))


def dot(a, b, dims):
    return lax.dot_general(a, b, dims, preferred_element_type=F32)


def pack_kernel(up_ref, final_ref, entry_ref, out_ref, entry_row):
    n_chip = out_ref.shape[0]
    entry_row[...] = jnp.zeros_like(entry_row)
    for t in range(9):
        out_ref[:, :, t * G : (t + 1) * G] = jnp.broadcast_to(final_ref[t][None], (n_chip, GD, G))
        entry_row[:, t * F : (t + 1) * F] = entry_ref[t].astype(F32)
    out_ref[:, :, L_FINAL:L_WEIGHTS] = jnp.broadcast_to(
        entry_row[...].astype(BF)[None], (n_chip, GD, L_ENTRY)
    )
    cols = up_ref.shape[2]
    lanes = 2 * n_chip * 128
    lane = lax.broadcasted_iota(jnp.int32, (cols, lanes), 1)
    col = lax.broadcasted_iota(jnp.int32, (cols, lanes), 0)
    want = (lane >> 7) * TILE_W - HALO + (lane & 31)
    hit = want == col
    block = (lane >> 5) & 3
    total = None
    for m in range(4):
        pick = jnp.where(hit & (block == m), 1.0, 0.0).astype(BF)
        rows = jnp.concatenate([up_ref[4 * k + m] for k in range(UP_H // 4)], axis=0)
        part = dot(rows, pick, NN)
        total = part if total is None else total + part
    total = total.astype(BF)
    for k in range(UP_H // 4):
        for d in range(2 * n_chip):
            start = L_WEIGHTS + L_UP * (d % 2) + 128 * k
            out_ref[d // 2, :, start : start + 128] = total[
                k * GD : (k + 1) * GD, 128 * d : 128 * (d + 1)
            ]


def px(first, last):
    return slice(first * FRAME_W, last * FRAME_W)


def main_kernel(
    n_row,
    pos_ref,
    pix_ref,
    w0_ref,
    w1_ref,
    w2_ref,
    mine_ref,
    other_ref,
    keep_ref,
    give_ref,
    valid,
    own,
    x0,
    x1,
    x2,
    x3,
    e3,
    up,
    k1,
    k2,
    k3,
    s1,
    s2,
    s3,
    s4,
    d4,
    d3,
    d2,
    wide,
    entry_out,
    stem_out,
):
    n_chip = mine_ref.shape[0]
    n_col = 2 * n_chip
    half = n_chip * GD
    core = pos_ref[1] & 1

    def both(first, last):
        return jnp.concatenate(
            [ref[:, :, first:last].reshape(half, last - first) for ref in (mine_ref, other_ref)], axis=0
        )

    cell = lax.broadcasted_iota(jnp.int32, (CELLS, 128), 0)
    row = (cell >> 5) - HALO + pos_ref[0] * TILE_H
    col_in = (cell & 31) - HALO
    col = col_in + pos_ref[1] * TILE_W
    inside = (row >= 0) & (row < n_row * TILE_H) & (col >= 0) & (col < n_col * TILE_W)
    valid[...] = jnp.where(inside, 1.0, 0.0)
    own[...] = jnp.where((col_in >= 0) & (col_in < TILE_W), 1.0, 0.0)

    def three(ref, first, last, value, width):
        n = value.shape[0]
        ref[px(first, last), 0:width] = pltpu.roll(value, 1, 0).astype(BF)
        ref[px(first, last), width : 2 * width] = value.astype(BF)
        ref[px(first, last), 2 * width : 3 * width] = pltpu.roll(value, n - 1, 0).astype(BF)

    def conv(ref, taps, first, last):
        return sum(dot(ref[px(first + p - 1, last + p - 1), :], taps[p], NT) for p in range(3))

    def act(pre, first, last):
        logistic = 1.0 / (1.0 + jnp.exp(-pre))
        width = pre.shape[1]
        mask = valid[px(first, last), :]
        mask = mask[:, :width] if width <= 128 else jnp.concatenate([mask] * (width // 128), axis=1)
        return pre * logistic * mask, logistic * (1.0 + pre * (1.0 - logistic)) * mask

    for p in range(3):
        for q in range(3):
            k1[p, :, q * F : (q + 1) * F] = w1_ref[3 * p + q]
            k2[p, :, q * F : (q + 1) * F] = w2_ref[3 * p + q]
        start = L_FINAL + 3 * F * p
        for j in range(n_chip):
            for ref, c in ((mine_ref, core), (other_ref, 1 - core)):
                at = pl.multiple_of((2 * j + c) * GD, GD)
                k3[p, pl.ds(at, GD), :] = ref[j, :, start : start + 3 * F]

    three(x0, 0, FRAME_H, jnp.transpose(pix_ref[...].astype(F32))[:CELLS], 16)
    a, s = act(conv(x0, [w0_ref[p] for p in range(3)], 1, 37), 1, 37)
    three(x1, 1, 37, a, F)
    s1[...] = s[px(6, 30), :]
    a, s = act(conv(x1, [k1[p] for p in range(3)], 2, 36), 2, 36)
    three(x2, 2, 36, a, F)
    s2[...] = s[px(4, 30), :]
    a, s = act(conv(x2, [k2[p] for p in range(3)], 3, 35), 3, 35)
    three(x3, 3, 35, a, F)
    s3[...] = s[px(2, 30), :]
    a, s = act(conv(x3, [k3[p] for p in range(3)], 4, 34), 4, 34)
    s4[...] = s
    n = a.shape[0]
    e3[0] = pltpu.roll(a, 1, 0).astype(BF)
    e3[1] = a.astype(BF)
    e3[2] = pltpu.roll(a, n - 1, 0).astype(BF)

    up_t = jnp.where(
        core == 0,
        both(L_WEIGHTS, L_WEIGHTS + L_UP).astype(F32),
        both(L_WEIGHTS + L_UP, L_SEND).astype(F32),
    )
    lane = lax.broadcasted_iota(jnp.int32, (n_col * GD, TILE_H * FRAME_W), 1) & 31
    mine = (lane >= HALO) & (lane < HALO + TILE_W)
    up_own = jnp.where(mine, up_t[:, 4 * FRAME_W : 28 * FRAME_W], 0.0).astype(BF)
    for p in range(3):
        for q in range(3):
            grad = dot(up_own, e3[q, px(2 + p, 26 + p), :], NN)
            grad = grad.astype(BF)
            for ref, first in ((keep_ref, 0), (give_ref, half)):
                for j in range(n_chip):
                    for h in range(2):
                        ref[j // 2, (j % 2) * T_GROUP + 2 * (3 * p + q) + h] = grad[
                            first + GD * j : first + GD * (j + 1), 128 * h : 128 * (h + 1)
                        ]

    up[...] = jnp.transpose(up_t).astype(BF)
    back = None
    for q in range(3):
        part = None
        for p in range(3):
            start = (3 * p + q) * G
            kernel = both(start, start + G)
            term = dot(up[px(2 - p, 32 - p), :], kernel, NN)
            part = term if part is None else part + term
        if q != 1:
            part = pltpu.roll(part, n - 1 if q == 0 else 1, 0)
        back = part if back is None else back + part
    d4[...] = (back * s4[...]).astype(BF)

    def masked(ref, offset):
        delta = ref[px(7 - offset, 31 - offset), :].astype(F32)
        mask = own[px(7, 31), :]
        width = delta.shape[1]
        mask = mask[:, :width] if width <= 128 else jnp.concatenate([mask] * (width // 128), axis=1)
        return (delta * mask).astype(BF)

    def grads(delta, ref):
        return [dot(delta, ref[px(6 + p, 30 + p), :], TN) for p in range(3)]

    def back_conv(ref, offset, taps, first, last):
        count = (last - first) * FRAME_W
        wide[0:count, :] = sum(
            dot(ref[px(first - p + 1 - offset, last - p + 1 - offset), :], taps[p], NN) for p in range(3)
        )
        return (
            pltpu.roll(wide[0:count, 0:F], count - 1, 0)
            + wide[0:count, F : 2 * F]
            + pltpu.roll(wide[0:count, 2 * F : 3 * F], 1, 0)
        )

    entry_out[...] = jnp.zeros_like(entry_out)
    for p, grad in enumerate(grads(masked(d4, 4), x3)):
        entry_out[:, 3 * F * p : 3 * F * (p + 1)] = grad
    for ref, c in ((keep_ref, core), (give_ref, 1 - core)):
        for j in range(n_chip):
            at = pl.multiple_of((2 * j + c) * GD, GD)
            for t in range(L_ENTRY // 128):
                ref[j // 2, (j % 2) * T_GROUP + L_FINAL // 128 + t] = entry_out[
                    pl.ds(at, GD), 128 * t : 128 * (t + 1)
                ].astype(BF)

    stem_out[...] = jnp.zeros_like(stem_out)
    d3[...] = (back_conv(d4, 4, [k3[p] for p in range(3)], 5, 33) * s3[...]).astype(BF)
    for p, grad in enumerate(grads(masked(d3, 5), x2)):
        stem_out[:, 576 + 192 * p : 768 + 192 * p] = grad
    d2[...] = (back_conv(d3, 5, [k2[p] for p in range(3)], 6, 32) * s2[...]).astype(BF)
    for p, grad in enumerate(grads(masked(d2, 6), x1)):
        stem_out[:, 192 * p : 192 + 192 * p] = grad
    d1 = back_conv(d2, 6, [k1[p] for p in range(3)], 7, 31) * s1[...]
    d1 = d1 * own[px(7, 31), :][:, :F]
    for p, grad in enumerate(grads(d1.astype(BF), x0)):
        stem_out[:, 1152 + 48 * p : 1200 + 48 * p] = grad
    for ref, c in ((keep_ref, core), (give_ref, 1 - core)):
        for g in range(2):
            at = pl.multiple_of(c * 32 + 16 * g, 16)
            for y in range(4):
                for t in range(3):
                    start = L_STEM * y + 128 * t
                    ref[y, 2 * T_GROUP + 3 * g + t] = stem_out[pl.ds(at, 16), start : start + 128].astype(BF)


def core_sum(pos_ref, keep_ref, got_ref, own_ref, up_ref, down_ref, far_ref):
    y = pos_ref[1] >> 2

    def total(index):
        return keep_ref[index].astype(F32) + got_ref[index].astype(F32)

    own_ref[...] = total(y)
    up_ref[...] = total((y + 1) & 3).astype(BF)
    down_ref[...] = total((y + 3) & 3).astype(BF)
    far_ref[...] = total((y + 2) & 3).astype(BF)


def four(own_ref, refs):
    total = own_ref[...]
    for ref in refs:
        total = total + ref[...].astype(F32)
    return total


def y_sum(pos_ref, own_ref, a_ref, b_ref, c_ref, z_ref, same_ref, flip_ref, total):
    z_hi = (pos_ref[1] >> 1) & 1
    total[...] = four(own_ref, (a_ref, b_ref, c_ref))
    stem = total[2 * T_GROUP :]
    group = total[pl.ds(z_hi * T_GROUP, T_GROUP)]
    z_ref[:T_GROUP] = group
    z_ref[T_GROUP:] = stem
    same_ref[:T_GROUP] = group.astype(BF)
    same_ref[T_GROUP:] = stem.astype(BF)
    flip_ref[:T_GROUP] = total[pl.ds((1 - z_hi) * T_GROUP, T_GROUP)].astype(BF)
    flip_ref[T_GROUP:] = stem.astype(BF)


def z_sum(own_ref, a_ref, b_ref, c_ref, x_ref, send_ref):
    total = four(own_ref, (a_ref, b_ref, c_ref))
    x_ref[...] = total
    send_ref[...] = total.astype(BF)


def x_sum(scale, own_ref, a_ref, b_ref, c_ref, final_ref, entry_ref, stem_ref):
    total = four(own_ref, (a_ref, b_ref, c_ref)) * scale
    for t in range(9):
        final_ref[t, :, 0:128] = total[2 * t]
        final_ref[t, :, 128:256] = total[2 * t + 1]
        entry_ref[t] = total[L_FINAL // 128 + t // 2][:, F * (t % 2) : F * (t % 2) + F]
    stem_ref[...] = total[T_GROUP:].astype(BF)


def stem_kernel(pos_ref, own_ref, a_ref, b_ref, c_ref, stem_ref, first_ref, second_ref, parts, whole):
    y = pos_ref[1] >> 2
    core = pos_ref[1] & 1
    for ref, offset in ((own_ref, 0), (a_ref, 3), (b_ref, 1), (c_ref, 2)):
        for k in range(2):
            parts[(y + offset) & 3, core if k == 0 else 1 - core] = ref[k].astype(F32)
    for at in range(4):
        for c in range(2):
            for g in range(2):
                for t in range(3):
                    first = 32 * c + 16 * g
                    start = L_STEM * at + 128 * t
                    whole[first : first + 16, start : start + 128] = parts[at, c, 3 * g + t]
    for t in range(9):
        first_ref[t] = whole[:, t * F : (t + 1) * F]
        second_ref[t] = whole[:, 576 + t * F : 576 + (t + 1) * F]
    for p in range(3):
        stem_ref[p] = whole[:, 1152 + 48 * p : 1200 + 48 * p]


def call(kernel, out_shape, scratch=(), n_in=1, smem=()):
    return pl.pallas_call(
        kernel,
        out_shape=out_shape,
        in_specs=[
            pl.BlockSpec(memory_space=pltpu.SMEM if i in smem else pltpu.VMEM) for i in range(n_in)
        ],
        out_specs=jax.tree.map(lambda _: pl.BlockSpec(memory_space=pltpu.VMEM), out_shape),
        scratch_shapes=list(scratch),
        compiler_params=pltpu.CompilerParams(vmem_limit_bytes=48 * 1024 * 1024),
    )


def rims(block, axis, dim, low, high):
    count = lax.axis_size(axis)
    forward = [(i, i + 1) for i in range(count - 1)]
    backward = [(target, source) for source, target in forward]
    size = block.shape[dim]
    before = lax.ppermute(lax.slice_in_dim(block, size - low, size, axis=dim), axis, forward)
    after = lax.ppermute(lax.slice_in_dim(block, 0, high, axis=dim), axis, backward)
    return jnp.concatenate([before, block, after], axis=dim)


def per_device(
    pixels, stem_weight, first_weight, second_weight, entry_weight, final_weight, upstream
):
    n_row = lax.axis_size("row")
    n_col = lax.axis_size("col")
    shape = jax.ShapeDtypeStruct
    scale = 1.0 / math.sqrt(TILE_H * n_row * TILE_W * n_col)
    pos = jnp.stack([lax.axis_index("row"), lax.axis_index("col")]).astype(jnp.int32)

    cells = pixels.astype(BF).reshape(3, TILE_H, 2, TILE_W, 2).transpose(0, 2, 4, 1, 3)
    cells = cells.reshape(12, TILE_H, TILE_W)
    cells = rims(cells, "row", 1, HALO, HALO)
    up_rows = rims(upstream, "row", 1, 4, 4).transpose(1, 0, 2)
    up_rows, cells = lax.optimization_barrier((up_rows, cells))
    cells = rims(cells, "col", 2, HALO, FRAME_W - TILE_W - HALO)
    cells = jnp.pad(cells.reshape(12, CELLS), ((0, 4), (0, 1280 - CELLS)))
    taps = lambda w: w.transpose(2, 3, 0, 1).reshape((9,) + w.shape[:2])
    send = call(
        pack_kernel,
        shape((n_col // 2, GD, L_SEND), BF),
        [pltpu.VMEM((GD, L_ENTRY), F32)],
        3,
    )(up_rows, taps(final_weight), taps(entry_weight))
    same_core = [[c for c in range(n_col) if c % 2 == k] for k in range(2)]
    sibling = [(c, c ^ 1) for c in range(n_col)]
    mine = lax.all_to_all(send, "col", 0, 0, tiled=True, axis_index_groups=same_core)
    other = lax.ppermute(mine, "col", sibling)

    w0 = jnp.pad(stem_weight, ((0, 0), (0, 0), (1, 1), (1, 1))).reshape(F, 3, 3, 2, 3, 2)
    w0 = w0.transpose(2, 0, 4, 1, 3, 5).reshape(3, F, 3, 12)
    w0 = jnp.pad(w0, ((0, 0), (0, 0), (0, 0), (0, 4))).reshape(3, F, 48)

    vmem = pltpu.VMEM
    half = shape((4, T_Y, 16, 128), BF)
    keep, give = call(
        functools.partial(main_kernel, n_row),
        (half, half),
        [
            vmem((CELLS, 128), F32),
            vmem((CELLS, 128), F32),
            vmem((CELLS, 48), BF),
            vmem((CELLS, 3 * F), BF),
            vmem((CELLS, 3 * F), BF),
            vmem((CELLS, 3 * F), BF),
            vmem((3, 30 * FRAME_W, G), BF),
            vmem((L_UP, G), BF),
            vmem((3, F, 3 * F), BF),
            vmem((3, F, 3 * F), BF),
            vmem((3, G, 3 * F), BF),
            vmem((24 * FRAME_W, F), F32),
            vmem((26 * FRAME_W, F), F32),
            vmem((28 * FRAME_W, F), F32),
            vmem((30 * FRAME_W, G), F32),
            vmem((30 * FRAME_W, G), BF),
            vmem((28 * FRAME_W, F), BF),
            vmem((26 * FRAME_W, F), BF),
            vmem((28 * FRAME_W, 3 * F), F32),
            vmem((G, L_ENTRY), F32),
            vmem((F, 4 * L_STEM), F32),
        ],
        7,
        (0,),
    )(pos, cells, w0, taps(first_weight), taps(second_weight), mine, other)

    def ring(axis, step, by):
        count = lax.axis_size(axis)
        return lambda value: lax.ppermute(value, axis, [(i, (i + step * by) % count) for i in range(count)])

    def flip(row_bit, col_bit):
        pairs = [
            (r * n_col + c, (r ^ row_bit) * n_col + (c ^ col_bit)) for r in range(n_row) for c in range(n_col)
        ]
        return lambda value: lax.ppermute(value, ("row", "col"), pairs)

    got = lax.ppermute(give, "col", sibling)
    y_bf, y_f32 = shape((T_Y, 16, 128), BF), shape((T_Y, 16, 128), F32)
    own, up, down, far = call(core_sum, (y_f32, y_bf, y_bf, y_bf), (), 3, (0,))(pos, keep, got)
    up, down, far = ring("col", 4, 1)(up), ring("col", 4, 3)(down), ring("col", 4, 2)(far)
    z_bf, z_f32 = shape((T_Z, 16, 128), BF), shape((T_Z, 16, 128), F32)
    own, same, other_z = call(y_sum, (z_f32, z_bf, z_bf), [vmem((T_Y, 16, 128), F32)], 5, (0,))(
        pos, own, up, down, far
    )
    same, hi, both_z = flip(1, 0)(same), flip(0, 2)(other_z), flip(1, 2)(other_z)
    own, send = call(z_sum, (z_f32, z_bf), (), 4)(own, same, hi, both_z)
    up, down, far = (ring("row", 2, k)(send) for k in (1, 3, 2))
    final_grad, entry_grad, stem_part = call(
        functools.partial(x_sum, scale),
        (shape((9, GD, G), F32), shape((9, GD, F), F32), shape((T_STEM, 16, 128), BF)),
        (),
        4,
    )(own, up, down, far)
    stem_pair = jnp.stack([stem_part, lax.ppermute(stem_part, "col", sibling)])
    up, down, far = (ring("col", 4, k)(stem_pair) for k in (1, 3, 2))
    stem_grad, first_grad, second_grad = call(
        stem_kernel,
        (shape((3, F, 48), F32), shape((9, F, F), F32), shape((9, F, F), F32)),
        [vmem((4, 2, T_STEM, 16, 128), F32), vmem((F, 4 * L_STEM), F32)],
        5,
        (0,),
    )(pos, stem_pair, up, down, far)

    untap = lambda g: g.reshape((3, 3) + g.shape[1:]).transpose(2, 3, 0, 1)
    stem_grad = stem_grad.reshape(3, F, 3, 16)[..., :12].reshape(3, F, 3, 3, 2, 2)
    stem_grad = stem_grad.transpose(1, 3, 0, 4, 2, 5).reshape(F, 3, 6, 6)[:, :, 1:5, 1:5]
    return (stem_grad, untap(first_grad), untap(second_grad), untap(entry_grad), untap(final_grad))


def solution(mesh):
    return jax.shard_map(
        per_device,
        mesh=mesh,
        in_specs=(
            P(None, "row", "col"),
            P(),
            P(),
            P(),
            P("col", None, None, None),
            P("col", None, None, None),
            P("col", "row", None),
        ),
        out_specs=(P(), P(), P(), P("col", None, None, None), P("col", None, None, None)),
        check_vma=False,
    )
```

```python
import functools
import math

import jax
import jax.numpy as jnp
import numpy as np
from jax import lax
from jax.experimental import pallas as pl
from jax.experimental.pallas import tpu as pltpu
from jax.sharding import PartitionSpec as P

BF = jnp.bfloat16
F32 = jnp.float32

TILE_H, TILE_W = 24, 16
HALO = 7
FRAME_H = TILE_H + 2 * HALO
FRAME_W = 32
CELLS = FRAME_H * FRAME_W
UP_H = TILE_H + 8
F = 64
G = 256
GD = 16
L_FINAL = 9 * G
L_ENTRY = 640
L_WEIGHTS = L_FINAL + L_ENTRY
L_UP = UP_H * FRAME_W
T_A = (0, 3, 4, 5, 6, 11)
T_B = (1, 7, 12)
T_P = (8, 9, 10)
T_TOP, T_BOTTOM = 2, 13
T_FIELD = 14
L_PIX = 640
RIM = 2 * HALO
T_GROUP = L_WEIGHTS // 128
T_STEM = 6
T_Y = 2 * T_GROUP + T_STEM
T_Z = T_GROUP + T_STEM
L_STEM = 384

NT = (((1,), (1,)), ((), ()))
NN = (((1,), (0,)), ((), ()))
TN = (((0,), (0,)), ((), ()))


def dot(a, b, dims):
    return lax.dot_general(a, b, dims, preferred_element_type=F32)


def pixel_planes(pix_ref):
    return [pix_ref[c, pl.ds(b, TILE_W, stride=2), :] for c in range(3) for b in range(2)]


def pack_kernel(up_ref, pix_ref, final_ref, entry_ref, out_ref, weight_ref, line):
    line[...] = jnp.zeros_like(line)
    for t in range(9):
        weight_ref[:, t * G : (t + 1) * G] = final_ref[t]
        line[:, t * F : (t + 1) * F] = entry_ref[t].astype(F32)
    weight_ref[:, L_FINAL:] = line[...].astype(BF)

    n_chip = out_ref.shape[0]
    cols = up_ref.shape[2]
    rows = [up_ref[r] for r in range(TILE_H)]
    lane = lax.broadcasted_iota(jnp.int32, (cols, 128 * n_chip), 1)
    col = lax.broadcasted_iota(jnp.int32, (cols, 128 * n_chip), 0)
    for width, skip, tiles in ((32, -HALO, T_A), (16, 32 - HALO, T_B)):
        per = 128 // width
        hit = (lane >> 7) * 2 * TILE_W + skip + (lane & (width - 1)) == col
        block = (lane & 127) // width
        total = None
        for m in range(per):
            pick = jnp.where(hit & (block == m), 1.0, 0.0).astype(BF)
            part = dot(jnp.concatenate(rows[m::per], axis=0), pick, NN)
            total = part if total is None else total + part
        total = total.astype(BF)
        for k, tile in enumerate(tiles):
            for d in range(n_chip):
                out_ref[d, tile] = total[k * GD : (k + 1) * GD, 128 * d : 128 * (d + 1)]
    line[...] = jnp.zeros_like(line)
    own = 2 * TILE_H
    for g, plane in enumerate(pixel_planes(pix_ref)):
        line[:, own * g : own * (g + 1)] = plane
        line[:, 384 + RIM * g : 384 + RIM * (g + 1)] = plane[:, :RIM]
        line[:, 512 + RIM * g : 512 + RIM * (g + 1)] = plane[:, own - RIM :]
    for k, tile in enumerate(T_P + (T_TOP, T_BOTTOM)):
        out_ref[:, tile] = jnp.broadcast_to(
            line[:, 128 * k : 128 * (k + 1)].astype(BF)[None], (n_chip, GD, 128)
        )


def pixel_pick():
    pick = np.zeros((L_PIX, 640), np.float32)
    own = 2 * TILE_H
    for i in range(FRAME_H):
        for c in range(3):
            for a in range(2):
                for b in range(2):
                    at, g = 2 * i + a, 2 * c + b
                    if at < RIM:
                        lane = 384 + RIM * g + at
                    elif at < RIM + own:
                        lane = own * g + at - RIM
                    else:
                        lane = 512 + RIM * g + at - RIM - own
                    pick[lane, 16 * i + 4 * c + 2 * a + b] = 1.0
    return jnp.asarray(pick, BF)


Y_STEPS = (0, 3, 1, 2)


def stem_rows():
    return [
        (p, 16 * q + 4 * c + 2 * a + b, c, 2 * p + a - 1, 2 * q + b - 1)
        for c in range(3)
        for p in range(3)
        for a in range(2)
        for q in range(3)
        for b in range(2)
        if 0 <= 2 * p + a - 1 < 4 and 0 <= 2 * q + b - 1 < 4
    ]


def px(first, last):
    return slice(first * FRAME_W, last * FRAME_W)


def main_kernel(
    n_row,
    pos_ref,
    pick_ref,
    w0_ref,
    w1_ref,
    w2_ref,
    wa_ref,
    wb_ref,
    wc_ref,
    wd_ref,
    mine_ref,
    other_ref,
    above_mine_ref,
    above_other_ref,
    below_mine_ref,
    below_other_ref,
    keep_ref,
    give_ref,
    valid,
    own,
    zone,
    x0f,
    x0,
    x1,
    x2,
    x3,
    e3,
    upt,
    up,
    k0,
    k1,
    k2,
    k3,
    s1,
    s2,
    s3,
    s4,
    d4,
    d3,
    d2,
    wide,
    entry_out,
    stem_out,
    stem_tiles,
):
    n_chip = mine_ref.shape[0]
    n_col = 2 * n_chip
    half = n_chip * GD
    core, z_hi, y = pos_ref[1] & 1, (pos_ref[1] >> 1) & 1, pos_ref[1] >> 2
    weights = (wa_ref, wb_ref, wc_ref, wd_ref)
    groups = []
    for c in (core, 1 - core):
        for z in (z_hi, 1 - z_hi):
            for step in Y_STEPS:
                groups.append((c, ((y + step) & 3) * 2 + z))

    def both(first, last):
        return jnp.concatenate(
            [ref[:, :, first:last].reshape(4 * GD, last - first) for ref in weights], axis=0
        )

    cell = lax.broadcasted_iota(jnp.int32, (CELLS, 128), 0)
    row = (cell >> 5) - HALO + pos_ref[0] * TILE_H
    col_in = (cell & 31) - HALO
    col = col_in + pos_ref[1] * TILE_W
    inside = (row >= 0) & (row < n_row * TILE_H) & (col >= 0) & (col < n_col * TILE_W)
    valid[...] = jnp.where(inside, 1.0, 0.0)
    own[...] = jnp.where((col_in >= 0) & (col_in < TILE_W), 1.0, 0.0)

    def three(ref, first, last, value, width):
        n = value.shape[0]
        ref[px(first, last), 0:width] = pltpu.roll(value, 1, 0).astype(BF)
        ref[px(first, last), width : 2 * width] = value.astype(BF)
        ref[px(first, last), 2 * width : 3 * width] = pltpu.roll(value, n - 1, 0).astype(BF)

    def conv(ref, taps, first, last):
        return sum(dot(ref[px(first + p - 1, last + p - 1), :], taps[p], NT) for p in range(3))

    def act(pre, first, last):
        logistic = 1.0 / (1.0 + jnp.exp(-pre))
        width = pre.shape[1]
        mask = valid[px(first, last), :]
        mask = mask[:, :width] if width <= 128 else jnp.concatenate([mask] * (width // 128), axis=1)
        return pre * logistic * mask, logistic * (1.0 + pre * (1.0 - logistic)) * mask

    for p in range(3):
        for q in range(3):
            k1[p, :, q * F : (q + 1) * F] = w1_ref[3 * p + q]
            k2[p, :, q * F : (q + 1) * F] = w2_ref[3 * p + q]
        start = L_FINAL + 3 * F * p
        for g, (c, chip) in enumerate(groups):
            at = pl.multiple_of((2 * chip + c) * GD, GD)
            k3[p, pl.ds(at, GD), :] = weights[g // 4][g % 4, :, start : start + 3 * F]

    tile = pos_ref[1]
    left = jnp.maximum(tile - 1, 0) >> 1
    right = jnp.minimum(tile + 1, n_col - 1) >> 1
    has_left = jnp.where(tile > 0, 1.0, 0.0)
    has_right = jnp.where(tile < n_col - 1, 1.0, 0.0)
    fields = (mine_ref, above_mine_ref, below_mine_ref), (other_ref, above_other_ref, below_other_ref)
    for (ref, above, below), chip, rows, skip, keep in (
        (fields[0], tile >> 1, slice(HALO, HALO + TILE_W), 0, None),
        (fields[1], left, slice(0, HALO), TILE_W - HALO, has_left),
        (fields[1], right, slice(HALO + TILE_W, FRAME_W), 0, has_right),
    ):
        parts = [ref[chip, t] for t in T_P] + [above[chip, 2], below[chip, 2]]
        for k, part in enumerate(parts):
            part = part.astype(F32)[skip : skip + rows.stop - rows.start]
            zone[rows, 128 * k : 128 * (k + 1)] = part if keep is None else part * keep
    spread = dot(zone[...].astype(BF), pick_ref[...], NN)
    for i in range(FRAME_H):
        x0f[px(i, i + 1), :] = spread[:, 16 * i : 16 * (i + 1)]
    three(x0, 0, FRAME_H, x0f[...], 16)
    k0[...] = jnp.zeros_like(k0)
    stem = w0_ref[...].astype(F32)
    for p, row, c, i, j in stem_rows():
        k0[p, row : row + 1, :] = stem[c, i, j : j + 1, :]
    a = sum(dot(x0[px(p, p + 36), :], k0[p].astype(BF), NN) for p in range(3))
    a, s = act(a, 1, 37)
    three(x1, 1, 37, a, F)
    s1[...] = s[px(6, 30), :]
    a, s = act(conv(x1, [k1[p] for p in range(3)], 2, 36), 2, 36)
    three(x2, 2, 36, a, F)
    s2[...] = s[px(4, 30), :]
    a, s = act(conv(x2, [k2[p] for p in range(3)], 3, 35), 3, 35)
    three(x3, 3, 35, a, F)
    s3[...] = s[px(2, 30), :]
    a, s = act(conv(x3, [k3[p] for p in range(3)], 4, 34), 4, 34)
    s4[...] = s
    n = a.shape[0]
    e3[0] = pltpu.roll(a, 1, 0).astype(BF)
    e3[1] = a.astype(BF)
    e3[2] = pltpu.roll(a, n - 1, 0).astype(BF)

    for g, (c, chip) in enumerate(groups):
        ref, above, below = fields[0 if g < n_chip else 1]
        parts = [above[chip, 0]] + [ref[chip, t] for t in T_A] + [below[chip, 0]]
        parts += [above[chip, 1]] + [ref[chip, t] for t in T_B] + [below[chip, 1]]
        for k, part in enumerate(parts):
            upt[g * GD : (g + 1) * GD, 128 * k : 128 * (k + 1)] = part.astype(F32)

    @pl.when(core == 1)
    def _():
        source = lax.broadcasted_iota(jnp.int32, (128, 256), 0)
        target = lax.broadcasted_iota(jnp.int32, (128, 256), 1)
        pick = (target >> 5 == source >> 4) & ((target & 31) == (source & 15) + 16)
        pick = jnp.where(pick, 1.0, 0.0).astype(BF)
        half_lane = lax.broadcasted_iota(jnp.int32, (n_col * GD, 128), 1) & 31
        for k in range(5):
            more = dot(upt[:, L_UP + 128 * k : L_UP + 128 * (k + 1)].astype(BF), pick, NN)
            for h in range(2):
                at = 2 * k + h - 1
                if 0 <= at < L_UP // 128:
                    now = slice(128 * at, 128 * (at + 1))
                    moved = pltpu.roll(upt[:, now], 112, 1)
                    upt[:, now] = jnp.where(half_lane < 16, moved, more[:, 128 * h : 128 * (h + 1)])

    up_t = upt[:, 0:L_UP]
    lane = lax.broadcasted_iota(jnp.int32, (n_col * GD, TILE_H * FRAME_W), 1) & 31
    mine = (lane >= HALO) & (lane < HALO + TILE_W)
    up_own = jnp.where(mine, up_t[:, 4 * FRAME_W : 28 * FRAME_W], 0.0).astype(BF)
    for p in range(3):
        for q in range(3):
            grad = dot(up_own, e3[q, px(2 + p, 26 + p), :], NN)
            grad = grad.astype(BF)
            for ref, first in ((keep_ref, 0), (give_ref, half)):
                for j in range(n_chip):
                    for h in range(2):
                        ref[j % 4, (j // 4) * T_GROUP + 2 * (3 * p + q) + h] = grad[
                            first + GD * j : first + GD * (j + 1), 128 * h : 128 * (h + 1)
                        ]

    up[...] = jnp.transpose(up_t).astype(BF)
    back = None
    for q in range(3):
        part = None
        for p in range(3):
            start = (3 * p + q) * G
            kernel = both(start, start + G)
            term = dot(up[px(2 - p, 32 - p), :], kernel, NN)
            part = term if part is None else part + term
        if q != 1:
            part = pltpu.roll(part, n - 1 if q == 0 else 1, 0)
        back = part if back is None else back + part
    d4[...] = (back * s4[...]).astype(BF)

    def masked(ref, offset):
        delta = ref[px(7 - offset, 31 - offset), :].astype(F32)
        mask = own[px(7, 31), :]
        width = delta.shape[1]
        mask = mask[:, :width] if width <= 128 else jnp.concatenate([mask] * (width // 128), axis=1)
        return (delta * mask).astype(BF)

    def grads(delta, ref):
        return [dot(delta, ref[px(6 + p, 30 + p), :], TN) for p in range(3)]

    def back_conv(ref, offset, taps, first, last):
        count = (last - first) * FRAME_W
        wide[0:count, :] = sum(
            dot(ref[px(first - p + 1 - offset, last - p + 1 - offset), :], taps[p], NN) for p in range(3)
        )
        return (
            pltpu.roll(wide[0:count, 0:F], count - 1, 0)
            + wide[0:count, F : 2 * F]
            + pltpu.roll(wide[0:count, 2 * F : 3 * F], 1, 0)
        )

    entry_out[...] = jnp.zeros_like(entry_out)
    for p, grad in enumerate(grads(masked(d4, 4), x3)):
        entry_out[:, 3 * F * p : 3 * F * (p + 1)] = grad
    for g, (c, chip) in enumerate(groups):
        ref, j = (keep_ref, g) if g < n_chip else (give_ref, g - n_chip)
        at = pl.multiple_of((2 * chip + c) * GD, GD)
        for t in range(L_ENTRY // 128):
            ref[j % 4, (j // 4) * T_GROUP + L_FINAL // 128 + t] = entry_out[
                pl.ds(at, GD), 128 * t : 128 * (t + 1)
            ].astype(BF)

    stem_out[...] = jnp.zeros_like(stem_out)
    d3[...] = (back_conv(d4, 4, [k3[p] for p in range(3)], 5, 33) * s3[...]).astype(BF)
    for p, grad in enumerate(grads(masked(d3, 5), x2)):
        stem_out[:, 576 + 192 * p : 768 + 192 * p] = grad
    d2[...] = (back_conv(d3, 5, [k2[p] for p in range(3)], 6, 32) * s2[...]).astype(BF)
    for p, grad in enumerate(grads(masked(d2, 6), x1)):
        stem_out[:, 192 * p : 192 + 192 * p] = grad
    d1 = back_conv(d2, 6, [k1[p] for p in range(3)], 7, 31) * s1[...]
    d1 = d1 * own[px(7, 31), :][:, :F]
    for p in range(3):
        stem_out[0:48, 1152 + F * p : 1152 + F * (p + 1)] = dot(
            x0[px(6 + p, 30 + p), :], d1.astype(BF), TN
        )
    for t in range(4 * L_STEM // 128):
        stem_tiles[t] = stem_out[:, 128 * t : 128 * (t + 1)]
    for ref, c in ((keep_ref, core), (give_ref, 1 - core)):
        for g in range(2):
            at = pl.multiple_of(c * 32 + 16 * g, 16)
            for k, step in enumerate(Y_STEPS):
                for t in range(3):
                    part = stem_tiles[((y + step) & 3) * 3 + t, pl.ds(at, 16), :]
                    ref[k, 2 * T_GROUP + 3 * g + t] = part.astype(BF)


def core_sum(keep_ref, got_ref, own_ref, *send_refs):
    own_ref[...] = keep_ref[0].astype(F32) + got_ref[0].astype(F32)
    for k, ref in enumerate(send_refs):
        ref[...] = (keep_ref[k + 1].astype(F32) + got_ref[k + 1].astype(F32)).astype(BF)


def four(own_ref, refs):
    total = own_ref[...]
    for ref in refs:
        total = total + ref[...].astype(F32)
    return total


def y_sum(own_ref, a_ref, b_ref, c_ref, z_ref, same_ref, flip_ref):
    total = four(own_ref, (a_ref, b_ref, c_ref))
    group, other, stem = total[:T_GROUP], total[T_GROUP : 2 * T_GROUP], total[2 * T_GROUP :]
    z_ref[:T_GROUP] = group
    z_ref[T_GROUP:] = stem
    same_ref[:T_GROUP] = group.astype(BF)
    same_ref[T_GROUP:] = stem.astype(BF)
    flip_ref[:T_GROUP] = other.astype(BF)
    flip_ref[T_GROUP:] = stem.astype(BF)


def z_sum(own_ref, a_ref, b_ref, c_ref, x_ref, send_ref):
    total = four(own_ref, (a_ref, b_ref, c_ref))
    x_ref[...] = total
    send_ref[...] = total.astype(BF)


def x_sum(scale, own_ref, a_ref, b_ref, c_ref, final_ref, entry_ref, stem_ref):
    total = four(own_ref, (a_ref, b_ref, c_ref)) * scale
    for t in range(9):
        final_ref[t, :, 0:128] = total[2 * t]
        final_ref[t, :, 128:256] = total[2 * t + 1]
        entry_ref[t] = total[L_FINAL // 128 + t // 2][:, F * (t % 2) : F * (t % 2) + F]
    stem_ref[...] = total[T_GROUP:].astype(BF)


def stem_kernel(pos_ref, own_ref, a_ref, b_ref, c_ref, stem_ref, first_ref, second_ref, parts, whole):
    y = pos_ref[1] >> 2
    core = pos_ref[1] & 1
    for ref, offset in ((own_ref, 0), (a_ref, 3), (b_ref, 1), (c_ref, 2)):
        for k in range(2):
            parts[(y + offset) & 3, core if k == 0 else 1 - core] = ref[k].astype(F32)
    for at in range(4):
        for c in range(2):
            for g in range(2):
                for t in range(3):
                    first = 32 * c + 16 * g
                    start = L_STEM * at + 128 * t
                    whole[first : first + 16, start : start + 128] = parts[at, c, 3 * g + t]
    for t in range(9):
        first_ref[t] = whole[:, t * F : (t + 1) * F]
        second_ref[t] = whole[:, 576 + t * F : 576 + (t + 1) * F]
    for p, row, c, i, j in stem_rows():
        stem_ref[c, i, j : j + 1, :] = whole[row : row + 1, 1152 + F * p : 1152 + F * (p + 1)]


def call(kernel, out_shape, scratch=(), n_in=1, smem=()):
    return pl.pallas_call(
        kernel,
        out_shape=out_shape,
        in_specs=[
            pl.BlockSpec(memory_space=pltpu.SMEM if i in smem else pltpu.VMEM) for i in range(n_in)
        ],
        out_specs=jax.tree.map(lambda _: pl.BlockSpec(memory_space=pltpu.VMEM), out_shape),
        scratch_shapes=list(scratch),
        compiler_params=pltpu.CompilerParams(vmem_limit_bytes=48 * 1024 * 1024),
    )


def per_device(
    pixels, stem_weight, first_weight, second_weight, entry_weight, final_weight, upstream
):
    n_row = lax.axis_size("row")
    n_col = lax.axis_size("col")
    shape = jax.ShapeDtypeStruct
    scale = 1.0 / math.sqrt(TILE_H * n_row * TILE_W * n_col)
    pos = jnp.stack([lax.axis_index("row"), lax.axis_index("col")]).astype(jnp.int32)

    def ring(axis, step, by):
        count = lax.axis_size(axis)
        return lambda value: lax.ppermute(value, axis, [(i, (i + step * by) % count) for i in range(count)])

    def flip(row_bit, col_bit):
        pairs = [
            (r * n_col + c, (r ^ row_bit) * n_col + (c ^ col_bit)) for r in range(n_row) for c in range(n_col)
        ]
        return lambda value: lax.ppermute(value, ("row", "col"), pairs)

    sibling = lambda value: lax.ppermute(value, "col", [(c, c ^ 1) for c in range(n_col)])
    y_ring = [ring("col", 4, step) for step in Y_STEPS[1:]]
    y_back = [ring("col", 4, 4 - step) for step in Y_STEPS[1:]]
    vmem = pltpu.VMEM
    taps = lambda w: w.transpose(2, 3, 0, 1).reshape((9,) + w.shape[:2])
    up_rows = upstream.transpose(1, 0, 2)
    pix = pixels.transpose(0, 2, 1)
    field, weight = call(
        pack_kernel,
        (shape((n_col // 2, T_FIELD, GD, 128), BF), shape((GD, L_WEIGHTS), BF)),
        [vmem((GD, L_PIX), F32)],
        4,
    )(up_rows, pix, taps(final_weight), taps(entry_weight))
    same_core = [[c for c in range(n_col) if c % 2 == k] for k in range(2)]
    mine = lax.all_to_all(field, "col", 0, 0, tiled=True, axis_index_groups=same_core)
    held = jnp.stack([weight] + [send(weight) for send in y_back])
    above = lax.ppermute(mine[:, T_FIELD - 3 :], "row", [(i, i + 1) for i in range(n_row - 1)])
    below = lax.ppermute(mine[:, :3], "row", [(i + 1, i) for i in range(n_row - 1)])
    held_z = flip(1, 2)(held)
    held_z, above, below = lax.optimization_barrier((held_z, above, below))
    held = [held, held_z, sibling(held), sibling(held_z)]
    field = [mine, sibling(mine), above, sibling(above), below, sibling(below)]

    half = shape((4, T_Y, 16, 128), BF)
    keep, give = call(
        functools.partial(main_kernel, n_row),
        (half, half),
        [
            vmem((CELLS, 128), F32),
            vmem((CELLS, 128), F32),
            vmem((FRAME_W, L_PIX), F32),
            vmem((CELLS, 16), F32),
            vmem((CELLS, 48), BF),
            vmem((CELLS, 3 * F), BF),
            vmem((CELLS, 3 * F), BF),
            vmem((CELLS, 3 * F), BF),
            vmem((3, 30 * FRAME_W, G), BF),
            vmem((G, L_UP + 5 * 128), F32),
            vmem((L_UP, G), BF),
            vmem((3, 48, F), F32),
            vmem((3, F, 3 * F), BF),
            vmem((3, F, 3 * F), BF),
            vmem((3, G, 3 * F), BF),
            vmem((24 * FRAME_W, F), F32),
            vmem((26 * FRAME_W, F), F32),
            vmem((28 * FRAME_W, F), F32),
            vmem((30 * FRAME_W, G), F32),
            vmem((30 * FRAME_W, G), BF),
            vmem((28 * FRAME_W, F), BF),
            vmem((26 * FRAME_W, F), BF),
            vmem((28 * FRAME_W, 3 * F), F32),
            vmem((G, L_ENTRY), F32),
            vmem((F, 4 * L_STEM), F32),
            vmem((12, F, 128), F32),
        ],
        15,
        (0,),
    )(pos, pixel_pick(), stem_weight.transpose(1, 2, 3, 0), taps(first_weight), taps(second_weight), *held, *field)

    got = sibling(give)
    y_bf, y_f32 = shape((T_Y, 16, 128), BF), shape((T_Y, 16, 128), F32)
    own, *parts = call(core_sum, (y_f32, y_bf, y_bf, y_bf), (), 2)(keep, got)
    parts = [send(part) for send, part in zip(y_ring, parts)]
    z_bf, z_f32 = shape((T_Z, 16, 128), BF), shape((T_Z, 16, 128), F32)
    own, same, other_z = call(y_sum, (z_f32, z_bf, z_bf), (), 4)(own, *parts)
    parts = flip(1, 0)(same), flip(0, 2)(other_z), flip(1, 2)(other_z)
    own, part = call(z_sum, (z_f32, z_bf), (), 4)(own, *parts)
    up, down, far = (ring("row", 2, k)(part) for k in (1, 3, 2))
    final_grad, entry_grad, stem_part = call(
        functools.partial(x_sum, scale),
        (shape((9, GD, G), F32), shape((9, GD, F), F32), shape((T_STEM, 16, 128), BF)),
        (),
        4,
    )(own, up, down, far)
    stem_pair = jnp.stack([stem_part, sibling(stem_part)])
    up, down, far = (ring("col", 4, k)(stem_pair) for k in (1, 3, 2))
    stem_grad, first_grad, second_grad = call(
        stem_kernel,
        (shape((3, 4, 4, F), F32), shape((9, F, F), F32), shape((9, F, F), F32)),
        [vmem((4, 2, T_STEM, 16, 128), F32), vmem((F, 4 * L_STEM), F32)],
        5,
        (0,),
    )(pos, stem_pair, up, down, far)

    untap = lambda g: g.reshape((3, 3) + g.shape[1:]).transpose(2, 3, 0, 1)
    stem_grad = stem_grad.transpose(3, 0, 1, 2)
    return (stem_grad, untap(first_grad), untap(second_grad), untap(entry_grad), untap(final_grad))


def solution(mesh):
    return jax.shard_map(
        per_device,
        mesh=mesh,
        in_specs=(
            P(None, "row", "col"),
            P(),
            P(),
            P(),
            P("col", None, None, None),
            P("col", None, None, None),
            P("col", "row", None),
        ),
        out_specs=(P(), P(), P(), P("col", None, None, None), P("col", None, None, None)),
        check_vma=False,
    )
```

```python
import functools
import math

import jax
import jax.numpy as jnp
import numpy as np
from jax import lax
from jax.experimental import pallas as pl
from jax.experimental.pallas import tpu as pltpu
from jax.sharding import PartitionSpec as P

BF = jnp.bfloat16
F32 = jnp.float32

TILE_H, TILE_W = 24, 16
HALO = 7
FRAME_H = TILE_H + 2 * HALO
FRAME_W = 32
CELLS = FRAME_H * FRAME_W
UP_H = TILE_H + 8
F = 64
G = 256
GD = 16
L_FINAL = 9 * G
L_ENTRY = 640
L_WEIGHTS = L_FINAL + L_ENTRY
L_UP = UP_H * FRAME_W
T_A = (0, 3, 4, 5, 6, 11)
T_B = (1, 7, 12)
T_P = (8, 9, 10)
T_TOP, T_BOTTOM = 2, 13
T_FIELD = 14
L_PIX = 640
RIM = 2 * HALO
T_GROUP = L_WEIGHTS // 128
T_STEM = 6
T_Y = 2 * T_GROUP + T_STEM
T_Z = T_GROUP + T_STEM
L_STEM = 384

NT = (((1,), (1,)), ((), ()))
NN = (((1,), (0,)), ((), ()))
TN = (((0,), (0,)), ((), ()))


def dot(a, b, dims):
    return lax.dot_general(a, b, dims, preferred_element_type=F32)


def pixel_planes(pix_ref):
    return [pix_ref[c, pl.ds(b, TILE_W, stride=2), :] for c in range(3) for b in range(2)]


def pack_kernel(up_ref, pix_ref, final_ref, entry_ref, out_ref, weight_ref, line):
    line[...] = jnp.zeros_like(line)
    for t in range(9):
        weight_ref[:, t * G : (t + 1) * G] = final_ref[t]
        line[:, t * F : (t + 1) * F] = entry_ref[t].astype(F32)
    weight_ref[:, L_FINAL:] = line[...].astype(BF)

    n_chip = out_ref.shape[0]
    cols = up_ref.shape[2]
    rows = [up_ref[r] for r in range(TILE_H)]
    lane = lax.broadcasted_iota(jnp.int32, (cols, 128 * n_chip), 1)
    col = lax.broadcasted_iota(jnp.int32, (cols, 128 * n_chip), 0)
    for width, skip, tiles in ((32, -HALO, T_A), (16, 32 - HALO, T_B)):
        per = 128 // width
        hit = (lane >> 7) * 2 * TILE_W + skip + (lane & (width - 1)) == col
        pick = jnp.where(hit, 1.0, 0.0).astype(BF)
        groups = [row for m in range(per) for row in rows[m::per]]
        windows = dot(jnp.concatenate(groups, axis=0), pick, NN)
        size = TILE_H // per * GD
        total = None
        for m in range(per):
            part = windows[m * size : (m + 1) * size]
            block = (lax.broadcasted_iota(jnp.int32, part.shape, 1) & 127) >> (width.bit_length() - 1)
            total = part if total is None else jnp.where(block == m, part, total)
        total = total.astype(BF)
        for k, tile in enumerate(tiles):
            for d in range(n_chip):
                out_ref[d, tile] = total[k * GD : (k + 1) * GD, 128 * d : 128 * (d + 1)]
    line[...] = jnp.zeros_like(line)
    own = 2 * TILE_H
    for g, plane in enumerate(pixel_planes(pix_ref)):
        line[:, own * g : own * (g + 1)] = plane
        line[:, 384 + RIM * g : 384 + RIM * (g + 1)] = plane[:, :RIM]
        line[:, 512 + RIM * g : 512 + RIM * (g + 1)] = plane[:, own - RIM :]
    for k, tile in enumerate(T_P + (T_TOP, T_BOTTOM)):
        out_ref[:, tile] = jnp.broadcast_to(
            line[:, 128 * k : 128 * (k + 1)].astype(BF)[None], (n_chip, GD, 128)
        )


def pixel_pick():
    pick = np.zeros((L_PIX, 640), np.float32)
    own = 2 * TILE_H
    for i in range(FRAME_H):
        for c in range(3):
            for a in range(2):
                for b in range(2):
                    at, g = 2 * i + a, 2 * c + b
                    if at < RIM:
                        lane = 384 + RIM * g + at
                    elif at < RIM + own:
                        lane = own * g + at - RIM
                    else:
                        lane = 512 + RIM * g + at - RIM - own
                    pick[lane, 16 * i + 4 * c + 2 * a + b] = 1.0
    return jnp.asarray(pick, BF)


Y_STEPS = (0, 3, 1, 2)


def stem_rows():
    return [
        (p, 16 * q + 4 * c + 2 * a + b, c, 2 * p + a - 1, 2 * q + b - 1)
        for c in range(3)
        for p in range(3)
        for a in range(2)
        for q in range(3)
        for b in range(2)
        if 0 <= 2 * p + a - 1 < 4 and 0 <= 2 * q + b - 1 < 4
    ]


def px(first, last):
    return slice(first * FRAME_W, last * FRAME_W)


def main_kernel(
    n_row,
    pos_ref,
    pick_ref,
    w0_ref,
    w1_ref,
    w2_ref,
    wa_ref,
    wb_ref,
    wc_ref,
    wd_ref,
    mine_ref,
    other_ref,
    above_mine_ref,
    above_other_ref,
    below_mine_ref,
    below_other_ref,
    keep_ref,
    give_ref,
    valid,
    own,
    zone,
    x0f,
    x0,
    x1,
    x2,
    x3,
    e3,
    upt,
    up,
    k0,
    k1,
    k2,
    k3,
    s1,
    s2,
    s3,
    s4,
    d4,
    d3,
    d2,
    wide,
    entry_out,
    stem_out,
    stem_tiles,
):
    n_chip = mine_ref.shape[0]
    n_col = 2 * n_chip
    half = n_chip * GD
    core, z_hi, y = pos_ref[1] & 1, (pos_ref[1] >> 1) & 1, pos_ref[1] >> 2
    weights = (wa_ref, wb_ref, wc_ref, wd_ref)
    groups = []
    for c in (core, 1 - core):
        for z in (z_hi, 1 - z_hi):
            for step in Y_STEPS:
                groups.append((c, ((y + step) & 3) * 2 + z))

    def both(first, last):
        return jnp.concatenate(
            [ref[:, :, first:last].reshape(4 * GD, last - first) for ref in weights], axis=0
        )

    cell = lax.broadcasted_iota(jnp.int32, (CELLS, 128), 0)
    row = (cell >> 5) + (pos_ref[0] * TILE_H - HALO)
    col_in = (cell & 31) - HALO
    col = col_in + pos_ref[1] * TILE_W
    inside = (row >= 0) & (row < n_row * TILE_H) & (col >= 0) & (col < n_col * TILE_W)
    valid[...] = jnp.where(inside, 1.0, 0.0)
    own[...] = jnp.where((col_in >= 0) & (col_in < TILE_W), 1.0, 0.0)

    def three(ref, first, last, value, width):
        n = value.shape[0]
        ref[px(first, last), 0:width] = pltpu.roll(value, 1, 0).astype(BF)
        ref[px(first, last), width : 2 * width] = value.astype(BF)
        ref[px(first, last), 2 * width : 3 * width] = pltpu.roll(value, n - 1, 0).astype(BF)

    def conv(ref, taps, first, last):
        return sum(dot(ref[px(first + p - 1, last + p - 1), :], taps[p], NT) for p in range(3))

    def act(pre, first, last):
        logistic = 1.0 / (1.0 + jnp.exp(-pre))
        width = pre.shape[1]
        mask = valid[px(first, last), :]
        mask = mask[:, :width] if width <= 128 else jnp.concatenate([mask] * (width // 128), axis=1)
        return pre * logistic * mask, logistic * (1.0 + pre * (1.0 - logistic)) * mask

    for p in range(3):
        for q in range(3):
            k1[p, :, q * F : (q + 1) * F] = w1_ref[3 * p + q]
            k2[p, :, q * F : (q + 1) * F] = w2_ref[3 * p + q]
        start = L_FINAL + 3 * F * p
        for g, (c, chip) in enumerate(groups):
            at = pl.multiple_of((2 * chip + c) * GD, GD)
            k3[p, pl.ds(at, GD), :] = weights[g // 4][g % 4, :, start : start + 3 * F]

    tile = pos_ref[1]
    left = jnp.maximum(tile - 1, 0) >> 1
    right = jnp.minimum(tile + 1, n_col - 1) >> 1
    has_left = jnp.where(tile > 0, 1.0, 0.0)
    has_right = jnp.where(tile < n_col - 1, 1.0, 0.0)
    fields = (mine_ref, above_mine_ref, below_mine_ref), (other_ref, above_other_ref, below_other_ref)
    for (ref, above, below), chip, rows, skip, keep in (
        (fields[0], tile >> 1, slice(HALO, HALO + TILE_W), 0, None),
        (fields[1], left, slice(0, HALO), TILE_W - HALO, has_left),
        (fields[1], right, slice(HALO + TILE_W, FRAME_W), 0, has_right),
    ):
        parts = [ref[chip, t] for t in T_P] + [above[chip, 2], below[chip, 2]]
        for k, part in enumerate(parts):
            part = part.astype(F32)[skip : skip + rows.stop - rows.start]
            zone[rows, 128 * k : 128 * (k + 1)] = part if keep is None else part * keep
    spread = dot(zone[...].astype(BF), pick_ref[...], NN)
    for i in range(FRAME_H):
        x0f[px(i, i + 1), :] = spread[:, 16 * i : 16 * (i + 1)]
    three(x0, 0, FRAME_H, x0f[...], 16)
    k0[...] = jnp.zeros_like(k0)
    stem = w0_ref[...].astype(F32)
    for p, row, c, i, j in stem_rows():
        k0[p, row : row + 1, :] = stem[c, i, j : j + 1, :]
    a = sum(dot(x0[px(p, p + 36), :], k0[p].astype(BF), NN) for p in range(3))
    a, s = act(a, 1, 37)
    three(x1, 1, 37, a, F)
    s1[...] = s[px(6, 30), :]
    a, s = act(conv(x1, [k1[p] for p in range(3)], 2, 36), 2, 36)
    three(x2, 2, 36, a, F)
    s2[...] = s[px(4, 30), :]
    a, s = act(conv(x2, [k2[p] for p in range(3)], 3, 35), 3, 35)
    three(x3, 3, 35, a, F)
    s3[...] = s[px(2, 30), :]
    a, s = act(conv(x3, [k3[p] for p in range(3)], 4, 34), 4, 34)
    s4[...] = s
    n = a.shape[0]
    e3[0] = pltpu.roll(a, 1, 0).astype(BF)
    e3[1] = a.astype(BF)
    e3[2] = pltpu.roll(a, n - 1, 0).astype(BF)

    for g, (c, chip) in enumerate(groups):
        ref, above, below = fields[0 if g < n_chip else 1]
        parts = [above[chip, 0]] + [ref[chip, t] for t in T_A] + [below[chip, 0]]
        parts += [above[chip, 1]] + [ref[chip, t] for t in T_B] + [below[chip, 1]]
        for k, part in enumerate(parts):
            upt[g * GD : (g + 1) * GD, 128 * k : 128 * (k + 1)] = part.astype(F32)

    @pl.when(core == 1)
    def _():
        source = lax.broadcasted_iota(jnp.int32, (128, 256), 0)
        target = lax.broadcasted_iota(jnp.int32, (128, 256), 1)
        pick = (target >> 5 == source >> 4) & ((target & 31) == (source & 15) + 16)
        pick = jnp.where(pick, 1.0, 0.0).astype(BF)
        half_lane = lax.broadcasted_iota(jnp.int32, (n_col * GD, 128), 1) & 31
        for k in range(5):
            more = dot(upt[:, L_UP + 128 * k : L_UP + 128 * (k + 1)].astype(BF), pick, NN)
            for h in range(2):
                at = 2 * k + h - 1
                if 0 <= at < L_UP // 128:
                    now = slice(128 * at, 128 * (at + 1))
                    moved = pltpu.roll(upt[:, now], 112, 1)
                    upt[:, now] = jnp.where(half_lane < 16, moved, more[:, 128 * h : 128 * (h + 1)])

    up_t = upt[:, 0:L_UP]
    lane = lax.broadcasted_iota(jnp.int32, (n_col * GD, TILE_H * FRAME_W), 1) & 31
    mine = (lane >= HALO) & (lane < HALO + TILE_W)
    up_own = jnp.where(mine, up_t[:, 4 * FRAME_W : 28 * FRAME_W], 0.0).astype(BF)
    for p in range(3):
        for q in range(3):
            grad = dot(up_own, e3[q, px(2 + p, 26 + p), :], NN)
            grad = grad.astype(BF)
            for ref, first in ((keep_ref, 0), (give_ref, half)):
                for j in range(n_chip):
                    for h in range(2):
                        ref[j % 4, (j // 4) * T_GROUP + 2 * (3 * p + q) + h] = grad[
                            first + GD * j : first + GD * (j + 1), 128 * h : 128 * (h + 1)
                        ]

    up[...] = jnp.transpose(up_t).astype(BF)
    back = None
    for q in range(3):
        part = None
        for p in range(3):
            start = (3 * p + q) * G
            kernel = both(start, start + G)
            term = dot(up[px(2 - p, 32 - p), :], kernel, NN)
            part = term if part is None else part + term
        if q != 1:
            part = pltpu.roll(part, n - 1 if q == 0 else 1, 0)
        back = part if back is None else back + part
    d4[...] = (back * s4[...]).astype(BF)

    def masked(ref, offset):
        delta = ref[px(7 - offset, 31 - offset), :].astype(F32)
        mask = own[px(7, 31), :]
        width = delta.shape[1]
        mask = mask[:, :width] if width <= 128 else jnp.concatenate([mask] * (width // 128), axis=1)
        return (delta * mask).astype(BF)

    def grads(delta, ref):
        return [dot(delta, ref[px(6 + p, 30 + p), :], TN) for p in range(3)]

    def back_conv(ref, offset, taps, first, last):
        count = (last - first) * FRAME_W
        wide[0:count, :] = sum(
            dot(ref[px(first - p + 1 - offset, last - p + 1 - offset), :], taps[p], NN) for p in range(3)
        )
        return (
            pltpu.roll(wide[0:count, 0:F], count - 1, 0)
            + wide[0:count, F : 2 * F]
            + pltpu.roll(wide[0:count, 2 * F : 3 * F], 1, 0)
        )

    entry_out[...] = jnp.zeros_like(entry_out)
    for p, grad in enumerate(grads(masked(d4, 4), x3)):
        entry_out[:, 3 * F * p : 3 * F * (p + 1)] = grad
    for g, (c, chip) in enumerate(groups):
        ref, j = (keep_ref, g) if g < n_chip else (give_ref, g - n_chip)
        at = pl.multiple_of((2 * chip + c) * GD, GD)
        for t in range(L_ENTRY // 128):
            ref[j % 4, (j // 4) * T_GROUP + L_FINAL // 128 + t] = entry_out[
                pl.ds(at, GD), 128 * t : 128 * (t + 1)
            ].astype(BF)

    stem_out[...] = jnp.zeros_like(stem_out)
    d3[...] = (back_conv(d4, 4, [k3[p] for p in range(3)], 5, 33) * s3[...]).astype(BF)
    for p, grad in enumerate(grads(masked(d3, 5), x2)):
        stem_out[:, 576 + 192 * p : 768 + 192 * p] = grad
    d2[...] = (back_conv(d3, 5, [k2[p] for p in range(3)], 6, 32) * s2[...]).astype(BF)
    for p, grad in enumerate(grads(masked(d2, 6), x1)):
        stem_out[:, 192 * p : 192 + 192 * p] = grad
    d1 = back_conv(d2, 6, [k1[p] for p in range(3)], 7, 31) * s1[...]
    d1 = d1 * own[px(7, 31), :][:, :F]
    for p in range(3):
        stem_out[0:48, 1152 + F * p : 1152 + F * (p + 1)] = dot(
            x0[px(6 + p, 30 + p), :], d1.astype(BF), TN
        )
    for t in range(4 * L_STEM // 128):
        stem_tiles[t] = stem_out[:, 128 * t : 128 * (t + 1)]
    for ref, c in ((keep_ref, core), (give_ref, 1 - core)):
        for g in range(2):
            at = pl.multiple_of(c * 32 + 16 * g, 16)
            for k, step in enumerate(Y_STEPS):
                for t in range(3):
                    part = stem_tiles[((y + step) & 3) * 3 + t, pl.ds(at, 16), :]
                    ref[k, 2 * T_GROUP + 3 * g + t] = part.astype(BF)


def core_sum(keep_ref, got_ref, own_ref, *send_refs):
    own_ref[...] = keep_ref[0].astype(F32) + got_ref[0].astype(F32)
    for k, ref in enumerate(send_refs):
        ref[...] = (keep_ref[k + 1].astype(F32) + got_ref[k + 1].astype(F32)).astype(BF)


def four(own_ref, refs):
    total = own_ref[...]
    for ref in refs:
        total = total + ref[...].astype(F32)
    return total


def y_sum(own_ref, a_ref, b_ref, c_ref, z_ref, same_ref, flip_ref):
    total = four(own_ref, (a_ref, b_ref, c_ref))
    group, other, stem = total[:T_GROUP], total[T_GROUP : 2 * T_GROUP], total[2 * T_GROUP :]
    z_ref[:T_GROUP] = group
    z_ref[T_GROUP:] = stem
    same_ref[:T_GROUP] = group.astype(BF)
    same_ref[T_GROUP:] = stem.astype(BF)
    flip_ref[:T_GROUP] = other.astype(BF)
    flip_ref[T_GROUP:] = stem.astype(BF)


def z_sum(own_ref, a_ref, b_ref, c_ref, x_ref, send_ref):
    total = four(own_ref, (a_ref, b_ref, c_ref))
    x_ref[...] = total
    send_ref[...] = total.astype(BF)


def x_sum(scale, own_ref, a_ref, b_ref, c_ref, final_ref, entry_ref, stem_ref):
    total = four(own_ref, (a_ref, b_ref, c_ref)) * scale
    for t in range(9):
        final_ref[t, :, 0:128] = total[2 * t]
        final_ref[t, :, 128:256] = total[2 * t + 1]
        entry_ref[t] = total[L_FINAL // 128 + t // 2][:, F * (t % 2) : F * (t % 2) + F]
    stem_ref[...] = total[T_GROUP:].astype(BF)


def stem_kernel(pos_ref, own_ref, a_ref, b_ref, c_ref, stem_ref, first_ref, second_ref, parts, whole):
    y = pos_ref[1] >> 2
    core = pos_ref[1] & 1
    for ref, offset in ((own_ref, 0), (a_ref, 3), (b_ref, 1), (c_ref, 2)):
        for k in range(2):
            parts[(y + offset) & 3, core if k == 0 else 1 - core] = ref[k].astype(F32)
    for at in range(4):
        for c in range(2):
            for g in range(2):
                for t in range(3):
                    first = 32 * c + 16 * g
                    start = L_STEM * at + 128 * t
                    whole[first : first + 16, start : start + 128] = parts[at, c, 3 * g + t]
    for t in range(9):
        first_ref[t] = whole[:, t * F : (t + 1) * F]
        second_ref[t] = whole[:, 576 + t * F : 576 + (t + 1) * F]
    for p, row, c, i, j in stem_rows():
        stem_ref[c, i, j : j + 1, :] = whole[row : row + 1, 1152 + F * p : 1152 + F * (p + 1)]


def call(kernel, out_shape, scratch=(), n_in=1, smem=()):
    return pl.pallas_call(
        kernel,
        out_shape=out_shape,
        in_specs=[
            pl.BlockSpec(memory_space=pltpu.SMEM if i in smem else pltpu.VMEM) for i in range(n_in)
        ],
        out_specs=jax.tree.map(lambda _: pl.BlockSpec(memory_space=pltpu.VMEM), out_shape),
        scratch_shapes=list(scratch),
        compiler_params=pltpu.CompilerParams(vmem_limit_bytes=48 * 1024 * 1024),
    )


def per_device(
    pixels, stem_weight, first_weight, second_weight, entry_weight, final_weight, upstream
):
    n_row = lax.axis_size("row")
    n_col = lax.axis_size("col")
    shape = jax.ShapeDtypeStruct
    scale = 1.0 / math.sqrt(TILE_H * n_row * TILE_W * n_col)
    pos = jnp.stack([lax.axis_index("row"), lax.axis_index("col")]).astype(jnp.int32)

    def ring(axis, step, by):
        count = lax.axis_size(axis)
        return lambda value: lax.ppermute(value, axis, [(i, (i + step * by) % count) for i in range(count)])

    def flip(row_bit, col_bit):
        pairs = [
            (r * n_col + c, (r ^ row_bit) * n_col + (c ^ col_bit)) for r in range(n_row) for c in range(n_col)
        ]
        return lambda value: lax.ppermute(value, ("row", "col"), pairs)

    sibling = lambda value: lax.ppermute(value, "col", [(c, c ^ 1) for c in range(n_col)])
    y_ring = [ring("col", 4, step) for step in Y_STEPS[1:]]
    y_back = [ring("col", 4, 4 - step) for step in Y_STEPS[1:]]
    vmem = pltpu.VMEM
    taps = lambda w: w.transpose(2, 3, 0, 1).reshape((9,) + w.shape[:2])
    up_rows = upstream.transpose(1, 0, 2)
    pix = pixels.transpose(0, 2, 1)
    field, weight = call(
        pack_kernel,
        (shape((n_col // 2, T_FIELD, GD, 128), BF), shape((GD, L_WEIGHTS), BF)),
        [vmem((GD, L_PIX), F32)],
        4,
    )(up_rows, pix, taps(final_weight), taps(entry_weight))
    same_core = [[c for c in range(n_col) if c % 2 == k] for k in range(2)]
    mine = lax.all_to_all(field, "col", 0, 0, tiled=True, axis_index_groups=same_core)
    held = jnp.stack([weight] + [send(weight) for send in y_back])
    above = lax.ppermute(mine[:, T_FIELD - 3 :], "row", [(i, i + 1) for i in range(n_row - 1)])
    below = lax.ppermute(mine[:, :3], "row", [(i + 1, i) for i in range(n_row - 1)])
    held_z = flip(1, 2)(held)
    held_z, above, below = lax.optimization_barrier((held_z, above, below))
    held = [held, held_z, sibling(held), sibling(held_z)]
    field = [mine, sibling(mine), above, sibling(above), below, sibling(below)]

    half = shape((4, T_Y, 16, 128), BF)
    keep, give = call(
        functools.partial(main_kernel, n_row),
        (half, half),
        [
            vmem((CELLS, 128), F32),
            vmem((CELLS, 128), F32),
            vmem((FRAME_W, L_PIX), F32),
            vmem((CELLS, 16), F32),
            vmem((CELLS, 48), BF),
            vmem((CELLS, 3 * F), BF),
            vmem((CELLS, 3 * F), BF),
            vmem((CELLS, 3 * F), BF),
            vmem((3, 30 * FRAME_W, G), BF),
            vmem((G, L_UP + 5 * 128), F32),
            vmem((L_UP, G), BF),
            vmem((3, 48, F), F32),
            vmem((3, F, 3 * F), BF),
            vmem((3, F, 3 * F), BF),
            vmem((3, G, 3 * F), BF),
            vmem((24 * FRAME_W, F), F32),
            vmem((26 * FRAME_W, F), F32),
            vmem((28 * FRAME_W, F), F32),
            vmem((30 * FRAME_W, G), F32),
            vmem((30 * FRAME_W, G), BF),
            vmem((28 * FRAME_W, F), BF),
            vmem((26 * FRAME_W, F), BF),
            vmem((28 * FRAME_W, 3 * F), F32),
            vmem((G, L_ENTRY), F32),
            vmem((F, 4 * L_STEM), F32),
            vmem((12, F, 128), F32),
        ],
        15,
        (0,),
    )(pos, pixel_pick(), stem_weight.transpose(1, 2, 3, 0), taps(first_weight), taps(second_weight), *held, *field)

    got = sibling(give)
    y_bf, y_f32 = shape((T_Y, 16, 128), BF), shape((T_Y, 16, 128), F32)
    own, *parts = call(core_sum, (y_f32, y_bf, y_bf, y_bf), (), 2)(keep, got)
    parts = [send(part) for send, part in zip(y_ring, parts)]
    z_bf, z_f32 = shape((T_Z, 16, 128), BF), shape((T_Z, 16, 128), F32)
    own, same, other_z = call(y_sum, (z_f32, z_bf, z_bf), (), 4)(own, *parts)
    parts = flip(1, 0)(same), flip(0, 2)(other_z), flip(1, 2)(other_z)
    own, part = call(z_sum, (z_f32, z_bf), (), 4)(own, *parts)
    up, down, far = (ring("row", 2, k)(part) for k in (1, 3, 2))
    final_grad, entry_grad, stem_part = call(
        functools.partial(x_sum, scale),
        (shape((9, GD, G), F32), shape((9, GD, F), F32), shape((T_STEM, 16, 128), BF)),
        (),
        4,
    )(own, up, down, far)
    stem_pair = jnp.stack([stem_part, sibling(stem_part)])
    up, down, far = (ring("col", 4, k)(stem_pair) for k in (1, 3, 2))
    stem_grad, first_grad, second_grad = call(
        stem_kernel,
        (shape((3, 4, 4, F), F32), shape((9, F, F), F32), shape((9, F, F), F32)),
        [vmem((4, 2, T_STEM, 16, 128), F32), vmem((F, 4 * L_STEM), F32)],
        5,
        (0,),
    )(pos, stem_pair, up, down, far)

    untap = lambda g: g.reshape((3, 3) + g.shape[1:]).transpose(2, 3, 0, 1)
    stem_grad = stem_grad.transpose(3, 0, 1, 2)
    return (stem_grad, untap(first_grad), untap(second_grad), untap(entry_grad), untap(final_grad))


def solution(mesh):
    return jax.shard_map(
        per_device,
        mesh=mesh,
        in_specs=(
            P(None, "row", "col"),
            P(),
            P(),
            P(),
            P("col", None, None, None),
            P("col", None, None, None),
            P("col", "row", None),
        ),
        out_specs=(P(), P(), P(), P("col", None, None, None), P("col", None, None, None)),
        check_vma=False,
    )
```

```python
import functools
import math

import jax
import jax.numpy as jnp
import numpy as np
from jax import lax
from jax.experimental import pallas as pl
from jax.experimental.pallas import tpu as pltpu
from jax.sharding import PartitionSpec as P

BF = jnp.bfloat16
F32 = jnp.float32

TILE_H, TILE_W = 24, 16
HALO = 7
FRAME_H = TILE_H + 2 * HALO
FRAME_W = 32
CELLS = FRAME_H * FRAME_W
UP_H = TILE_H + 8
F = 64
G = 256
GD = 16
L_FINAL = 9 * G
L_ENTRY = 640
L_WEIGHTS = L_FINAL + L_ENTRY
L_UP = UP_H * FRAME_W
T_A = (0, 3, 4, 5, 6, 9)
T_B = (1, 7, 10)
T_P = (2, 8, 11)
T_FIELD = 12
L_PIX = 640
RIM = 2 * HALO
T_GROUP = L_WEIGHTS // 128
T_STEM = 6
T_Y = 2 * T_GROUP + T_STEM
T_Z = T_GROUP + T_STEM
L_STEM = 384

NT = (((1,), (1,)), ((), ()))
NN = (((1,), (0,)), ((), ()))
TN = (((0,), (0,)), ((), ()))


def dot(a, b, dims):
    return lax.dot_general(a, b, dims, preferred_element_type=F32)


def pixel_planes(pix_ref):
    return [pix_ref[c, pl.ds(b, TILE_W, stride=2), :] for c in range(3) for b in range(2)]


def pack_kernel(up_ref, pix_ref, final_ref, entry_ref, out_ref, weight_ref, line):
    line[...] = jnp.zeros_like(line)
    for t in range(9):
        weight_ref[:, t * G : (t + 1) * G] = final_ref[t]
        line[:, t * F : (t + 1) * F] = entry_ref[t].astype(F32)
    weight_ref[:, L_FINAL:] = line[...].astype(BF)

    n_chip = out_ref.shape[0]
    cols = up_ref.shape[2]
    rows = [up_ref[r] for r in range(TILE_H)]
    lane = lax.broadcasted_iota(jnp.int32, (cols, 128 * n_chip), 1)
    col = lax.broadcasted_iota(jnp.int32, (cols, 128 * n_chip), 0)
    for width, skip, tiles in ((32, -HALO, T_A), (16, 32 - HALO, T_B)):
        per = 128 // width
        hit = (lane >> 7) * 2 * TILE_W + skip + (lane & (width - 1)) == col
        pick = jnp.where(hit, 1.0, 0.0).astype(BF)
        groups = [row for m in range(per) for row in rows[m::per]]
        windows = dot(jnp.concatenate(groups, axis=0), pick, NN)
        size = TILE_H // per * GD
        total = None
        for m in range(per):
            part = windows[m * size : (m + 1) * size]
            block = (lax.broadcasted_iota(jnp.int32, part.shape, 1) & 127) >> (width.bit_length() - 1)
            total = part if total is None else jnp.where(block == m, part, total)
        total = total.astype(BF)
        for k, tile in enumerate(tiles):
            for d in range(n_chip):
                out_ref[d, tile] = total[k * GD : (k + 1) * GD, 128 * d : 128 * (d + 1)]
    line[...] = jnp.zeros_like(line)
    own = 2 * TILE_H
    middle = own - 2 * RIM
    for g, plane in enumerate(pixel_planes(pix_ref)):
        line[:, RIM * g : RIM * (g + 1)] = plane[:, :RIM]
        line[:, 128 + middle * g : 128 + middle * (g + 1)] = plane[:, RIM : own - RIM]
        line[:, 256 + RIM * g : 256 + RIM * (g + 1)] = plane[:, own - RIM :]
    for k, tile in enumerate(T_P):
        out_ref[:, tile] = jnp.broadcast_to(
            line[:, 128 * k : 128 * (k + 1)].astype(BF)[None], (n_chip, GD, 128)
        )


def pixel_pick():
    pick = np.zeros((L_PIX, 640), np.float32)
    own = 2 * TILE_H
    for i in range(FRAME_H):
        for c in range(3):
            for a in range(2):
                for b in range(2):
                    at, g = 2 * i + a, 2 * c + b
                    row = at - RIM
                    if row < 0:
                        lane = 384 + RIM * g + at
                    elif row < RIM:
                        lane = RIM * g + row
                    elif row < own - RIM:
                        lane = 128 + (own - 2 * RIM) * g + row - RIM
                    elif row < own:
                        lane = 256 + RIM * g + row - own + RIM
                    else:
                        lane = 512 + RIM * g + row - own
                    pick[lane, 16 * i + 4 * c + 2 * a + b] = 1.0
    return jnp.asarray(pick, BF)


Y_STEPS = (0, 3, 1, 2)


def stem_rows():
    return [
        (p, 16 * q + 4 * c + 2 * a + b, c, 2 * p + a - 1, 2 * q + b - 1)
        for c in range(3)
        for p in range(3)
        for a in range(2)
        for q in range(3)
        for b in range(2)
        if 0 <= 2 * p + a - 1 < 4 and 0 <= 2 * q + b - 1 < 4
    ]


def px(first, last):
    return slice(first * FRAME_W, last * FRAME_W)


def main_kernel(
    n_row,
    pos_ref,
    pick_ref,
    w0_ref,
    w1_ref,
    w2_ref,
    wa_ref,
    wb_ref,
    wc_ref,
    wd_ref,
    mine_ref,
    other_ref,
    above_mine_ref,
    above_other_ref,
    below_mine_ref,
    below_other_ref,
    keep_ref,
    give_ref,
    valid,
    own,
    zone,
    x0f,
    x0,
    x1,
    x2,
    x3,
    e3,
    upt,
    up,
    k0,
    k1,
    k2,
    k3,
    s1,
    s2,
    s3,
    s4,
    d4,
    d3,
    d2,
    wide,
    entry_out,
    stem_out,
    stem_tiles,
):
    n_chip = mine_ref.shape[0]
    n_col = 2 * n_chip
    half = n_chip * GD
    core, z_hi, y = pos_ref[1] & 1, (pos_ref[1] >> 1) & 1, pos_ref[1] >> 2
    weights = (wa_ref, wb_ref, wc_ref, wd_ref)
    groups = []
    for c in (core, 1 - core):
        for z in (z_hi, 1 - z_hi):
            for step in Y_STEPS:
                groups.append((c, ((y + step) & 3) * 2 + z))

    def both(first, last):
        return jnp.concatenate(
            [ref[:, :, first:last].reshape(4 * GD, last - first) for ref in weights], axis=0
        )

    cell = lax.broadcasted_iota(jnp.int32, (CELLS, 128), 0)
    row = (cell >> 5) + (pos_ref[0] * TILE_H - HALO)
    col_in = (cell & 31) - HALO
    col = col_in + pos_ref[1] * TILE_W
    inside = (row >= 0) & (row < n_row * TILE_H) & (col >= 0) & (col < n_col * TILE_W)
    valid[...] = jnp.where(inside, 1.0, 0.0)
    own[...] = jnp.where((col_in >= 0) & (col_in < TILE_W), 1.0, 0.0)

    def three(ref, first, last, value, width):
        n = value.shape[0]
        ref[px(first, last), 0:width] = pltpu.roll(value, 1, 0).astype(BF)
        ref[px(first, last), width : 2 * width] = value.astype(BF)
        ref[px(first, last), 2 * width : 3 * width] = pltpu.roll(value, n - 1, 0).astype(BF)

    def conv(ref, taps, first, last):
        return sum(dot(ref[px(first + p - 1, last + p - 1), :], taps[p], NT) for p in range(3))

    def act(pre, first, last):
        logistic = 1.0 / (1.0 + jnp.exp(-pre))
        width = pre.shape[1]
        mask = valid[px(first, last), :]
        mask = mask[:, :width] if width <= 128 else jnp.concatenate([mask] * (width // 128), axis=1)
        return pre * logistic * mask, logistic * (1.0 + pre * (1.0 - logistic)) * mask

    for p in range(3):
        for q in range(3):
            k1[p, :, q * F : (q + 1) * F] = w1_ref[3 * p + q]
            k2[p, :, q * F : (q + 1) * F] = w2_ref[3 * p + q]
        start = L_FINAL + 3 * F * p
        for g, (c, chip) in enumerate(groups):
            at = pl.multiple_of((2 * chip + c) * GD, GD)
            k3[p, pl.ds(at, GD), :] = weights[g // 4][g % 4, :, start : start + 3 * F]

    tile = pos_ref[1]
    left = jnp.maximum(tile - 1, 0) >> 1
    right = jnp.minimum(tile + 1, n_col - 1) >> 1
    has_left = jnp.where(tile > 0, 1.0, 0.0)
    has_right = jnp.where(tile < n_col - 1, 1.0, 0.0)
    fields = (mine_ref, above_mine_ref, below_mine_ref), (other_ref, above_other_ref, below_other_ref)
    for (ref, above, below), chip, rows, skip, keep in (
        (fields[0], tile >> 1, slice(HALO, HALO + TILE_W), 0, None),
        (fields[1], left, slice(0, HALO), TILE_W - HALO, has_left),
        (fields[1], right, slice(HALO + TILE_W, FRAME_W), 0, has_right),
    ):
        parts = [ref[chip, t] for t in T_P] + [above[chip, 2], below[chip, 2]]
        for k, part in enumerate(parts):
            part = part.astype(F32)[skip : skip + rows.stop - rows.start]
            zone[rows, 128 * k : 128 * (k + 1)] = part if keep is None else part * keep
    spread = dot(zone[...].astype(BF), pick_ref[...], NN)
    for i in range(FRAME_H):
        x0f[px(i, i + 1), :] = spread[:, 16 * i : 16 * (i + 1)]
    three(x0, 0, FRAME_H, x0f[...], 16)
    k0[...] = jnp.zeros_like(k0)
    stem = w0_ref[...].astype(F32)
    for p, row, c, i, j in stem_rows():
        k0[p, row : row + 1, :] = stem[c, i, j : j + 1, :]
    a = sum(dot(x0[px(p, p + 36), :], k0[p].astype(BF), NN) for p in range(3))
    a, s = act(a, 1, 37)
    three(x1, 1, 37, a, F)
    s1[...] = s[px(6, 30), :]
    a, s = act(conv(x1, [k1[p] for p in range(3)], 2, 36), 2, 36)
    three(x2, 2, 36, a, F)
    s2[...] = s[px(4, 30), :]
    a, s = act(conv(x2, [k2[p] for p in range(3)], 3, 35), 3, 35)
    three(x3, 3, 35, a, F)
    s3[...] = s[px(2, 30), :]
    a, s = act(conv(x3, [k3[p] for p in range(3)], 4, 34), 4, 34)
    s4[...] = s
    n = a.shape[0]
    e3[0] = pltpu.roll(a, 1, 0).astype(BF)
    e3[1] = a.astype(BF)
    e3[2] = pltpu.roll(a, n - 1, 0).astype(BF)

    for g, (c, chip) in enumerate(groups):
        ref, above, below = fields[0 if g < n_chip else 1]
        parts = [above[chip, 0]] + [ref[chip, t] for t in T_A] + [below[chip, 0]]
        parts += [above[chip, 1]] + [ref[chip, t] for t in T_B] + [below[chip, 1]]
        for k, part in enumerate(parts):
            upt[g * GD : (g + 1) * GD, 128 * k : 128 * (k + 1)] = part.astype(F32)

    @pl.when(core == 1)
    def _():
        source = lax.broadcasted_iota(jnp.int32, (128, 256), 0)
        target = lax.broadcasted_iota(jnp.int32, (128, 256), 1)
        pick = (target >> 5 == source >> 4) & ((target & 31) == (source & 15) + 16)
        pick = jnp.where(pick, 1.0, 0.0).astype(BF)
        half_lane = lax.broadcasted_iota(jnp.int32, (n_col * GD, 128), 1) & 31
        for k in range(5):
            more = dot(upt[:, L_UP + 128 * k : L_UP + 128 * (k + 1)].astype(BF), pick, NN)
            for h in range(2):
                at = 2 * k + h - 1
                if 0 <= at < L_UP // 128:
                    now = slice(128 * at, 128 * (at + 1))
                    moved = pltpu.roll(upt[:, now], 112, 1)
                    upt[:, now] = jnp.where(half_lane < 16, moved, more[:, 128 * h : 128 * (h + 1)])

    up_t = upt[:, 0:L_UP]
    lane = lax.broadcasted_iota(jnp.int32, (n_col * GD, TILE_H * FRAME_W), 1) & 31
    mine = (lane >= HALO) & (lane < HALO + TILE_W)
    up_own = jnp.where(mine, up_t[:, 4 * FRAME_W : 28 * FRAME_W], 0.0).astype(BF)
    for p in range(3):
        for q in range(3):
            grad = dot(up_own, e3[q, px(2 + p, 26 + p), :], NN)
            grad = grad.astype(BF)
            for ref, first in ((keep_ref, 0), (give_ref, half)):
                for j in range(n_chip):
                    for h in range(2):
                        ref[j % 4, (j // 4) * T_GROUP + 2 * (3 * p + q) + h] = grad[
                            first + GD * j : first + GD * (j + 1), 128 * h : 128 * (h + 1)
                        ]

    up[...] = jnp.transpose(up_t).astype(BF)
    back = None
    for q in range(3):
        part = None
        for p in range(3):
            start = (3 * p + q) * G
            kernel = both(start, start + G)
            term = dot(up[px(2 - p, 32 - p), :], kernel, NN)
            part = term if part is None else part + term
        if q != 1:
            part = pltpu.roll(part, n - 1 if q == 0 else 1, 0)
        back = part if back is None else back + part
    d4[...] = (back * s4[...]).astype(BF)

    def masked(ref, offset):
        delta = ref[px(7 - offset, 31 - offset), :].astype(F32)
        mask = own[px(7, 31), :]
        width = delta.shape[1]
        mask = mask[:, :width] if width <= 128 else jnp.concatenate([mask] * (width // 128), axis=1)
        return (delta * mask).astype(BF)

    def grads(delta, ref):
        return [dot(delta, ref[px(6 + p, 30 + p), :], TN) for p in range(3)]

    def back_conv(ref, offset, taps, first, last):
        count = (last - first) * FRAME_W
        wide[0:count, :] = sum(
            dot(ref[px(first - p + 1 - offset, last - p + 1 - offset), :], taps[p], NN) for p in range(3)
        )
        return (
            pltpu.roll(wide[0:count, 0:F], count - 1, 0)
            + wide[0:count, F : 2 * F]
            + pltpu.roll(wide[0:count, 2 * F : 3 * F], 1, 0)
        )

    entry_out[...] = jnp.zeros_like(entry_out)
    for p, grad in enumerate(grads(masked(d4, 4), x3)):
        entry_out[:, 3 * F * p : 3 * F * (p + 1)] = grad
    for g, (c, chip) in enumerate(groups):
        ref, j = (keep_ref, g) if g < n_chip else (give_ref, g - n_chip)
        at = pl.multiple_of((2 * chip + c) * GD, GD)
        for t in range(L_ENTRY // 128):
            ref[j % 4, (j // 4) * T_GROUP + L_FINAL // 128 + t] = entry_out[
                pl.ds(at, GD), 128 * t : 128 * (t + 1)
            ].astype(BF)

    stem_out[...] = jnp.zeros_like(stem_out)
    d3[...] = (back_conv(d4, 4, [k3[p] for p in range(3)], 5, 33) * s3[...]).astype(BF)
    for p, grad in enumerate(grads(masked(d3, 5), x2)):
        stem_out[:, 576 + 192 * p : 768 + 192 * p] = grad
    d2[...] = (back_conv(d3, 5, [k2[p] for p in range(3)], 6, 32) * s2[...]).astype(BF)
    for p, grad in enumerate(grads(masked(d2, 6), x1)):
        stem_out[:, 192 * p : 192 + 192 * p] = grad
    d1 = back_conv(d2, 6, [k1[p] for p in range(3)], 7, 31) * s1[...]
    d1 = d1 * own[px(7, 31), :][:, :F]
    for p in range(3):
        stem_out[0:48, 1152 + F * p : 1152 + F * (p + 1)] = dot(
            x0[px(6 + p, 30 + p), :], d1.astype(BF), TN
        )
    for t in range(4 * L_STEM // 128):
        stem_tiles[t] = stem_out[:, 128 * t : 128 * (t + 1)]
    for ref, c in ((keep_ref, core), (give_ref, 1 - core)):
        for g in range(2):
            at = pl.multiple_of(c * 32 + 16 * g, 16)
            for k, step in enumerate(Y_STEPS):
                for t in range(3):
                    part = stem_tiles[((y + step) & 3) * 3 + t, pl.ds(at, 16), :]
                    ref[k, 2 * T_GROUP + 3 * g + t] = part.astype(BF)


def core_sum(keep_ref, got_ref, own_ref, *send_refs):
    own_ref[...] = keep_ref[0].astype(F32) + got_ref[0].astype(F32)
    for k, ref in enumerate(send_refs):
        ref[...] = (keep_ref[k + 1].astype(F32) + got_ref[k + 1].astype(F32)).astype(BF)


def four(own_ref, refs):
    total = own_ref[...]
    for ref in refs:
        total = total + ref[...].astype(F32)
    return total


def y_sum(own_ref, a_ref, b_ref, c_ref, z_ref, same_ref, flip_ref):
    total = four(own_ref, (a_ref, b_ref, c_ref))
    group, other, stem = total[:T_GROUP], total[T_GROUP : 2 * T_GROUP], total[2 * T_GROUP :]
    z_ref[:T_GROUP] = group
    z_ref[T_GROUP:] = stem
    same_ref[:T_GROUP] = group.astype(BF)
    same_ref[T_GROUP:] = stem.astype(BF)
    flip_ref[:T_GROUP] = other.astype(BF)
    flip_ref[T_GROUP:] = stem.astype(BF)


def z_sum(own_ref, a_ref, b_ref, c_ref, x_ref, send_ref):
    total = four(own_ref, (a_ref, b_ref, c_ref))
    x_ref[...] = total
    send_ref[...] = total.astype(BF)


def x_sum(scale, own_ref, a_ref, b_ref, c_ref, final_ref, entry_ref, stem_ref):
    total = four(own_ref, (a_ref, b_ref, c_ref)) * scale
    for t in range(9):
        final_ref[t, :, 0:128] = total[2 * t]
        final_ref[t, :, 128:256] = total[2 * t + 1]
        entry_ref[t] = total[L_FINAL // 128 + t // 2][:, F * (t % 2) : F * (t % 2) + F]
    stem_ref[...] = total[T_GROUP:].astype(BF)


def stem_kernel(pos_ref, own_ref, a_ref, b_ref, c_ref, stem_ref, first_ref, second_ref, parts, whole):
    y = pos_ref[1] >> 2
    core = pos_ref[1] & 1
    for ref, offset in ((own_ref, 0), (a_ref, 3), (b_ref, 1), (c_ref, 2)):
        for k in range(2):
            parts[(y + offset) & 3, core if k == 0 else 1 - core] = ref[k].astype(F32)
    for at in range(4):
        for c in range(2):
            for g in range(2):
                for t in range(3):
                    first = 32 * c + 16 * g
                    start = L_STEM * at + 128 * t
                    whole[first : first + 16, start : start + 128] = parts[at, c, 3 * g + t]
    for t in range(9):
        first_ref[t] = whole[:, t * F : (t + 1) * F]
        second_ref[t] = whole[:, 576 + t * F : 576 + (t + 1) * F]
    for p, row, c, i, j in stem_rows():
        stem_ref[c, i, j : j + 1, :] = whole[row : row + 1, 1152 + F * p : 1152 + F * (p + 1)]


def call(kernel, out_shape, scratch=(), n_in=1, smem=()):
    return pl.pallas_call(
        kernel,
        out_shape=out_shape,
        in_specs=[
            pl.BlockSpec(memory_space=pltpu.SMEM if i in smem else pltpu.VMEM) for i in range(n_in)
        ],
        out_specs=jax.tree.map(lambda _: pl.BlockSpec(memory_space=pltpu.VMEM), out_shape),
        scratch_shapes=list(scratch),
        compiler_params=pltpu.CompilerParams(vmem_limit_bytes=48 * 1024 * 1024),
    )


def per_device(
    pixels, stem_weight, first_weight, second_weight, entry_weight, final_weight, upstream
):
    n_row = lax.axis_size("row")
    n_col = lax.axis_size("col")
    shape = jax.ShapeDtypeStruct
    scale = 1.0 / math.sqrt(TILE_H * n_row * TILE_W * n_col)
    pos = jnp.stack([lax.axis_index("row"), lax.axis_index("col")]).astype(jnp.int32)

    def ring(axis, step, by):
        count = lax.axis_size(axis)
        return lambda value: lax.ppermute(value, axis, [(i, (i + step * by) % count) for i in range(count)])

    def flip(row_bit, col_bit):
        pairs = [
            (r * n_col + c, (r ^ row_bit) * n_col + (c ^ col_bit)) for r in range(n_row) for c in range(n_col)
        ]
        return lambda value: lax.ppermute(value, ("row", "col"), pairs)

    sibling = lambda value: lax.ppermute(value, "col", [(c, c ^ 1) for c in range(n_col)])
    y_ring = [ring("col", 4, step) for step in Y_STEPS[1:]]
    y_back = [ring("col", 4, 4 - step) for step in Y_STEPS[1:]]
    vmem = pltpu.VMEM
    taps = lambda w: w.transpose(2, 3, 0, 1).reshape((9,) + w.shape[:2])
    up_rows = upstream.transpose(1, 0, 2)
    pix = pixels.transpose(0, 2, 1)
    field, weight = call(
        pack_kernel,
        (shape((n_col // 2, T_FIELD, GD, 128), BF), shape((GD, L_WEIGHTS), BF)),
        [vmem((GD, L_PIX), F32)],
        4,
    )(up_rows, pix, taps(final_weight), taps(entry_weight))
    same_core = [[c for c in range(n_col) if c % 2 == k] for k in range(2)]
    mine = lax.all_to_all(field, "col", 0, 0, tiled=True, axis_index_groups=same_core)
    held = jnp.stack([weight] + [send(weight) for send in y_back])
    above = lax.ppermute(mine[:, T_FIELD - 3 :], "row", [(i, i + 1) for i in range(n_row - 1)])
    below = lax.ppermute(mine[:, :3], "row", [(i + 1, i) for i in range(n_row - 1)])
    held_z = flip(1, 2)(held)
    held_z, above, below = lax.optimization_barrier((held_z, above, below))
    held = [held, held_z, sibling(held), sibling(held_z)]
    field = [mine, sibling(mine), above, sibling(above), below, sibling(below)]

    half = shape((4, T_Y, 16, 128), BF)
    keep, give = call(
        functools.partial(main_kernel, n_row),
        (half, half),
        [
            vmem((CELLS, 128), F32),
            vmem((CELLS, 128), F32),
            vmem((FRAME_W, L_PIX), F32),
            vmem((CELLS, 16), F32),
            vmem((CELLS, 48), BF),
            vmem((CELLS, 3 * F), BF),
            vmem((CELLS, 3 * F), BF),
            vmem((CELLS, 3 * F), BF),
            vmem((3, 30 * FRAME_W, G), BF),
            vmem((G, L_UP + 5 * 128), F32),
            vmem((L_UP, G), BF),
            vmem((3, 48, F), F32),
            vmem((3, F, 3 * F), BF),
            vmem((3, F, 3 * F), BF),
            vmem((3, G, 3 * F), BF),
            vmem((24 * FRAME_W, F), F32),
            vmem((26 * FRAME_W, F), F32),
            vmem((28 * FRAME_W, F), F32),
            vmem((30 * FRAME_W, G), F32),
            vmem((30 * FRAME_W, G), BF),
            vmem((28 * FRAME_W, F), BF),
            vmem((26 * FRAME_W, F), BF),
            vmem((28 * FRAME_W, 3 * F), F32),
            vmem((G, L_ENTRY), F32),
            vmem((F, 4 * L_STEM), F32),
            vmem((12, F, 128), F32),
        ],
        15,
        (0,),
    )(pos, pixel_pick(), stem_weight.transpose(1, 2, 3, 0), taps(first_weight), taps(second_weight), *held, *field)

    got = sibling(give)
    y_bf, y_f32 = shape((T_Y, 16, 128), BF), shape((T_Y, 16, 128), F32)
    own, *parts = call(core_sum, (y_f32, y_bf, y_bf, y_bf), (), 2)(keep, got)
    parts = [send(part) for send, part in zip(y_ring, parts)]
    z_bf, z_f32 = shape((T_Z, 16, 128), BF), shape((T_Z, 16, 128), F32)
    own, same, other_z = call(y_sum, (z_f32, z_bf, z_bf), (), 4)(own, *parts)
    parts = flip(1, 0)(same), flip(0, 2)(other_z), flip(1, 2)(other_z)
    own, part = call(z_sum, (z_f32, z_bf), (), 4)(own, *parts)
    up, down, far = (ring("row", 2, k)(part) for k in (1, 3, 2))
    final_grad, entry_grad, stem_part = call(
        functools.partial(x_sum, scale),
        (shape((9, GD, G), F32), shape((9, GD, F), F32), shape((T_STEM, 16, 128), BF)),
        (),
        4,
    )(own, up, down, far)
    stem_pair = jnp.stack([stem_part, sibling(stem_part)])
    up, down, far = (ring("col", 4, k)(stem_pair) for k in (1, 3, 2))
    stem_grad, first_grad, second_grad = call(
        stem_kernel,
        (shape((3, 4, 4, F), F32), shape((9, F, F), F32), shape((9, F, F), F32)),
        [vmem((4, 2, T_STEM, 16, 128), F32), vmem((F, 4 * L_STEM), F32)],
        5,
        (0,),
    )(pos, stem_pair, up, down, far)

    untap = lambda g: g.reshape((3, 3) + g.shape[1:]).transpose(2, 3, 0, 1)
    stem_grad = stem_grad.transpose(3, 0, 1, 2)
    return (stem_grad, untap(first_grad), untap(second_grad), untap(entry_grad), untap(final_grad))


def solution(mesh):
    return jax.shard_map(
        per_device,
        mesh=mesh,
        in_specs=(
            P(None, "row", "col"),
            P(),
            P(),
            P(),
            P("col", None, None, None),
            P("col", None, None, None),
            P("col", "row", None),
        ),
        out_specs=(P(), P(), P(), P("col", None, None, None), P("col", None, None, None)),
        check_vma=False,
    )
```
